32 devices in a mesh: row: 8 (over z, y), col: 4 (over x, core).
Axes of the slice: x: 2, y: 2, z: 4, core: 2. Of those that a mesh axis runs over, the one named last changes fastest.
Arguments:
- row_embed: float32 [8192, 512], P(('row', 'col')), may hold values from -1.5 to 1.5
- row_accum: float32 [8192, 512], P(('row', 'col')), may hold values from 0.001 to 0.01
- col_embed: float32 [4, 4096, 512], P('col', 'row'), may hold values from -1.5 to 1.5
- col_accum: float32 [4, 4096, 512], P('col', 'row'), may hold values from 0.001 to 0.01
- col_freq: int32 [4, 4096], P('col'), may hold values from 1000 to 29999
- row_freq: int32 [8192], P('row'), may hold values from 1000 to 29999
- block_cols: int32 [8, 4, 2], P('row', 'col'), may hold values from 0 to 3, all different within a row
- counts: int32 [8, 4, 2, 1024, 1024], P('row', 'col'), may hold values from 0 to 1024
- excluded: int32 [512], replicated, may hold values from 0 to 8191
- log_total: float32 [], replicated, may hold values from 15 to 19
Outputs:
- row_embed_new: float32 [8192, 512], P(('row', 'col'))
- row_accum_new: float32 [8192, 512], P(('row', 'col'))
- col_embed_new: float32 [4, 4096, 512], P('col', 'row')
- col_accum_new: float32 [4, 4096, 512], P('col', 'row')
The draws below stay inside these ranges and needn't reach their ends.
Inputs may be any that keep to these rules, and one draw needn't show every extreme that they name: `block_cols`: the 2 column blocks of one row block and group are different.
All inputs are finite; a program needn't handle non-finite values.
Results may differ from the reference program's by a relative error of at most 0.0071.
The reference program's roundings to bfloat16 on the way (of `cell`) count: a program that leaves them out, or rounds other values in their place, can miss the bound.
Values may be sent and summed in bfloat16 or wider, within the bound.
No kernel may reach another device: no remote copies, remote signals or barrier semaphores. Data moves between devices by JAX's collectives and lax.ppermute only.
A program may use at most 128 MiB of HBM per device.

```python
import math
import jax
import jax.numpy as jnp
from jax import lax

D = 512
BLOCK = 1024
GROUP_BLOCKS = 4
SLOTS = 2
EXCLUDED = 512
ROW_BLOCKS = 8
GROUPS = 4
ROWS = 8192
GROUP_COLS = 4096


def draw_counts(key, part):
    shape = (ROW_BLOCKS, GROUPS, SLOTS, BLOCK, BLOCK)
    key_level = jax.random.fold_in(key, 11)
    key_value = jax.random.fold_in(key, 23)
    level = jax.random.randint(key_level, shape, -3, 11)
    ceiling = jnp.left_shift(jnp.int32(1), jnp.maximum(level, 0)) + 1
    value = jax.random.randint(key_value, shape, 1, ceiling)
    return jnp.where(level >= 0, value, 0).astype(jnp.int32)


def set_ends(result, rng, least, largest):
    longest = result.shape.index(max(result.shape))
    spots = []
    for shift in (0, 1):
        where = [jax.random.randint(jax.random.fold_in(rng, axis), (), 0, length) for axis, length in enumerate(result.shape)]
        where[longest] = (where[longest] + shift) % result.shape[longest]
        spots.append(tuple(where))
    return result.at[spots[0]].set(least).at[spots[1]].set(largest)


def block_levels(rng, shape, cuts, low, largest):
    loudness = 1.0
    for dim, blocks in cuts:
        heights = jax.random.uniform(jax.random.fold_in(jax.random.fold_in(rng, 6), dim), (blocks,), jnp.float32, low / len(cuts), largest / len(cuts))
        loudness = loudness * jnp.repeat(jnp.exp(heights), shape[dim] // blocks).reshape((-1,) + (1,) * (len(shape) - 1 - dim))
    return loudness


def different_ones(own_key, rows, amount, top, lift):
    sequence = jax.random.permutation(jax.random.fold_in(own_key, 1), amount)
    favour = sequence
    for power in range(3):
        favour = favour * favour // amount
    favour = favour * lift // amount
    chance = jax.random.randint(jax.random.fold_in(own_key, 2), (rows, amount), 0, 4096) + favour
    holders = jax.random.permutation(jax.random.fold_in(own_key, 3), rows)[jnp.arange(amount) % rows]
    chance = jnp.where(jnp.arange(rows)[:, None] == holders[None, :], 1 << 14, chance)
    score = chance * amount + jnp.arange(amount)
    return lax.top_k(score.astype(jnp.int32), top)[1].astype(jnp.int32)


def bell_draw(key, shape, scale, reach, cuts=(), held_as=jnp.bfloat16):
    drawn = scale * jax.random.normal(key, shape, jnp.float32)
    if cuts:
        drawn = drawn * block_levels(key, shape, cuts, -0.22, 0.18)
    return jnp.clip(drawn, -reach, reach).astype(held_as)


def setup_inputs(seed: int = 0) -> dict:
    key_of = jax.random.split(jax.random.key(seed), 11)
    return {
        "row_embed": bell_draw(key_of[0], (ROWS, D), 0.25, 1.5, ((0, 32),), jnp.float32),
        "row_accum": jnp.clip(jnp.exp(math.log(0.01) - 2.30258502 * jax.random.uniform(key_of[1], (ROWS, D), jnp.float32) ** block_levels(key_of[1], (ROWS, D), ((0, 32),), -0.2, 0.2)), 0.001, 0.01),
        "col_embed": bell_draw(key_of[2], (GROUPS, GROUP_COLS, D), 0.25, 1.5, ((0, 4), (1, 8)), jnp.float32),
        "col_accum": jnp.clip(jnp.exp(math.log(0.01) - 2.30258502 * jax.random.uniform(key_of[3], (GROUPS, GROUP_COLS, D), jnp.float32) ** block_levels(key_of[3], (GROUPS, GROUP_COLS, D), ((0, 4), (1, 8)), -0.2, 0.2)), 0.001, 0.01),
        "col_freq": set_ends(jax.random.randint(key_of[4], (GROUPS, GROUP_COLS), 1000, 30000), jax.random.fold_in(key_of[4], 1), 1000, 29999).astype(jnp.int32),
        "row_freq": set_ends(jax.random.randint(key_of[5], (ROWS,), 1000, 30000), jax.random.fold_in(key_of[5], 1), 1000, 29999).astype(jnp.int32),
        "block_cols": different_ones(key_of[6], ROW_BLOCKS * GROUPS, GROUP_BLOCKS, SLOTS, 4096).reshape((ROW_BLOCKS, GROUPS, SLOTS)),
        "counts": draw_counts(jax.random.fold_in(key_of[10], 71), 0),
        "excluded": set_ends(jax.random.randint(key_of[8], (EXCLUDED,), 0, ROWS), jax.random.fold_in(key_of[8], 1), 0, ROWS - 1).astype(jnp.int32),
        "log_total": jnp.clip(jax.random.uniform(key_of[9], (), jnp.float32, 15.0, 19.0), 15.0, 19.0),
    }


learn_rate = 0.2
decay_rate = 0.5

def cell_grads(count_block, predicted, row_logs, col_logs, log_total):
    nonzero = count_block > 0
    safe_count = jnp.where(nonzero, count_block.astype(jnp.float32), jnp.float32(1.0))
    baseline = log_total - row_logs[:, None] - col_logs[None, :]
    weight = 0.1 + 0.25 * jnp.sqrt(safe_count)
    fitted = weight * (predicted - baseline - jnp.log(safe_count))
    hinge_grad = jax.nn.sigmoid(predicted - baseline)
    return (jnp.where(nonzero, fitted, hinge_grad) / BLOCK).astype(jnp.bfloat16)

def reference(row_embed, row_accum, col_embed, col_accum, col_freq, row_freq, block_cols, counts, excluded, log_total):
    row_half = row_embed.astype(jnp.bfloat16)
    col_half = col_embed.astype(jnp.bfloat16)
    row_logs = jnp.log(row_freq.astype(jnp.float32))
    col_logs = jnp.log(col_freq.astype(jnp.float32))
    zero = jnp.int32(0)

    def one_block(step, gradients):
        row_grad, col_grad = gradients
        step = jnp.asarray(step).astype(jnp.int32)
        row_index = step // (GROUPS * SLOTS)
        group_index = step // SLOTS % GROUPS
        slot_index = step % SLOTS
        chosen = block_cols[row_index, group_index, slot_index].astype(jnp.int32)
        row_start = row_index * BLOCK
        col_start = chosen * BLOCK
        row_block = lax.dynamic_slice(row_half, (row_start, zero), (BLOCK, D))
        col_block = lax.dynamic_slice(col_half, (group_index, col_start, zero), (1, BLOCK, D))[0]
        block_row_logs = lax.dynamic_slice(row_logs, (row_start,), (BLOCK,))
        block_col_logs = lax.dynamic_slice(col_logs, (group_index, col_start), (1, BLOCK))[0]
        count_block = lax.dynamic_slice(counts, (row_index, group_index, slot_index, zero, zero), (1, 1, 1, BLOCK, BLOCK))[0, 0, 0]
        predicted = jnp.dot(row_block, col_block.T, preferred_element_type=jnp.float32)
        cell = cell_grads(count_block, predicted, block_row_logs, block_col_logs, log_total)
        row_part = jnp.dot(cell, col_block, preferred_element_type=jnp.float32)
        col_part = jnp.dot(cell.T, row_block, preferred_element_type=jnp.float32)
        old_rows = lax.dynamic_slice(row_grad, (row_start, zero), (BLOCK, D))
        row_grad = lax.dynamic_update_slice(row_grad, old_rows + row_part, (row_start, zero))
        old_cols = lax.dynamic_slice(col_grad, (group_index, col_start, zero), (1, BLOCK, D))
        col_grad = lax.dynamic_update_slice(col_grad, old_cols + col_part[None], (group_index, col_start, zero))
        return (row_grad, col_grad)
    start_rows = jnp.zeros((ROWS, D), jnp.float32)
    start_cols = jnp.zeros((GROUPS, GROUP_COLS, D), jnp.float32)
    row_grad, col_grad = lax.fori_loop(0, ROW_BLOCKS * GROUPS * SLOTS, one_block, (start_rows, start_cols))
    row_ids = jnp.arange(ROWS, dtype=jnp.int32)
    decayed = jnp.all(row_ids[:, None] != excluded[None, :], axis=1)
    freq_root = jnp.sqrt(row_freq.astype(jnp.float32))
    decay_coef = jnp.where(decayed, decay_rate * freq_root / (freq_root + 30.0), jnp.float32(0.0))
    full_grad = row_grad + decay_coef[:, None] * row_embed
    row_accum_new = row_accum + full_grad * full_grad
    row_embed_new = row_embed - learn_rate * full_grad / jnp.sqrt(row_accum_new)
    col_accum_new = col_accum + col_grad * col_grad
    col_embed_new = col_embed - learn_rate * col_grad / jnp.sqrt(col_accum_new)
    return (row_embed_new, row_accum_new, col_embed_new, col_accum_new)
```

```python
import functools

import jax
import jax.numpy as jnp
from jax import lax
from jax.experimental import pallas as pl
from jax.experimental.pallas import tpu as pltpu
from jax.sharding import PartitionSpec as P

learn_rate = 0.2
decay_rate = 0.5

PARTS = 2


def cell_grads(count_block, shifted, block):
    safe_count = jnp.maximum(count_block, 1).astype(jnp.float32)
    weight = (0.1 / block) + (0.25 / block) * jnp.sqrt(safe_count)
    fitted = weight * (shifted - jnp.log(safe_count))
    hinge_grad = (0.5 / block) * jnp.tanh(0.5 * shifted) + (0.5 / block)
    return jnp.where(count_block > 0, fitted, hinge_grad).astype(jnp.bfloat16)


def block_kernel(first, block, meta, own_rows, x_rows, core_rows, cols, row_term, col_term, counts, *rest):
    if first:
        row_grad, col_grad = rest
    else:
        row_before, row_grad, col_grad = rest
    slot = pl.program_id(0)
    some = cols[0]
    size = own_rows.shape[0]

    @pl.when(slot == 0)
    def _():
        if first:
            row_grad[...] = jnp.zeros_like(row_grad)
        else:
            row_grad[...] = row_before[...]

    total = None
    for piece in range(4):
        rows = (own_rows, core_rows.at[0], x_rows, core_rows.at[1])[piece][...]
        at = pl.ds(pl.multiple_of((meta[1] ^ piece) * size, size), size)
        predicted = lax.dot_general(
            rows, some, (((1,), (1,)), ((), ())), preferred_element_type=jnp.float32
        )
        shifted = predicted + row_term[at, :] + col_term[0]
        cell = cell_grads(counts[0, 0, 0, at, :], shifted, block)
        row_grad[piece] += jnp.dot(cell, some, preferred_element_type=jnp.float32)
        term = lax.dot_general(
            cell, rows, (((0,), (0,)), ((), ())), preferred_element_type=jnp.float32
        )
        total = term if total is None else total + term
    col_grad[0] = total.astype(col_grad.dtype)


def block_grads(meta, rows, cols, row_term, col_term, counts, row_before, col_type):
    own_rows, x_rows, core_rows = rows
    slots, span, width = cols.shape
    size = own_rows.shape[0]
    block = counts.shape[3]
    first = row_before is None
    whole2 = lambda slot, meta: (0, 0)
    whole3 = lambda slot, meta: (0, 0, 0)
    in_specs = [
        pl.BlockSpec((size, width), whole2),
        pl.BlockSpec((size, width), whole2),
        pl.BlockSpec((2, size, width), whole3),
        pl.BlockSpec((1, span, width), lambda slot, meta: (slot, 0, 0)),
        pl.BlockSpec((block, 1), whole2),
        pl.BlockSpec((1, 1, span), lambda slot, meta: (slot, 0, 0)),
        pl.BlockSpec((1, 1, 1, block, span), lambda slot, meta: (0, 0, slot, 0, meta[0])),
    ]
    args = [own_rows, x_rows, core_rows, cols, row_term, col_term, counts]
    if not first:
        in_specs.append(pl.BlockSpec((4, size, width), whole3))
        args.append(row_before)
    return pl.pallas_call(
        functools.partial(block_kernel, first, block),
        grid_spec=pltpu.PrefetchScalarGridSpec(
            num_scalar_prefetch=1,
            grid=(slots,),
            in_specs=in_specs,
            out_specs=[
                pl.BlockSpec((4, size, width), whole3),
                pl.BlockSpec((1, span, width), lambda slot, meta: (slot, 0, 0)),
            ],
        ),
        out_shape=[
            jax.ShapeDtypeStruct((4, size, width), jnp.float32),
            jax.ShapeDtypeStruct((slots, span, width), col_type),
        ],
        cost_estimate=pl.CostEstimate(
            flops=6 * slots * block * span * width,
            bytes_accessed=slots * block * span * 4 + 3 * block * width * 4,
            transcendentals=3 * slots * block * span,
        ),
        compiler_params=pltpu.CompilerParams(vmem_limit_bytes=40 * 1024 * 1024),
    )(meta, *args)


def crossed_body(
    row_embed,
    row_accum,
    col_embed,
    col_accum,
    col_freq,
    row_freq,
    block_cols,
    counts,
    excluded,
    log_total,
):
    block = counts.shape[3]
    slots = counts.shape[2]
    own_rows = row_embed.shape[0]
    own_cols = col_embed.shape[1]
    span = own_cols // PARTS
    row_index = lax.axis_index("row")
    col_index = lax.axis_index("col")
    half = row_index % 2
    home = row_index // 2
    edge = (home == 0) | (home == 3)

    mate_swap = [(i, i ^ 1) for i in range(8)]
    near_swap = [(i, i ^ 2) for i in range(8)]
    far_swap = [(i, i ^ 4) for i in range(8)]
    inner_swap = [(i, i ^ 6) for i in range(2, 6)]
    to_edge = [(i, i ^ 2) for i in range(2, 6)]
    from_edge = [(i, i ^ 2) for i in (0, 1, 6, 7)]
    core_swap = [(i, i ^ 1) for i in range(4)]
    chip_swap = [(i, i ^ 2) for i in range(4)]

    chosen = block_cols[0, 0]
    mate_chosen = lax.ppermute(chosen, "row", mate_swap)

    row_half = row_embed.astype(jnp.bfloat16)
    col_half = col_embed[0].astype(jnp.bfloat16)

    gathered = []
    for part in range(PARTS):
        own = col_half[part * span : (part + 1) * span]
        near = lax.ppermute(own, "row", near_swap)
        far = lax.ppermute(own, "row", far_swap)
        inner = lax.ppermute(own, "row", inner_swap)
        last = lax.ppermute(far, "row", to_edge)
        gathered.append((own, near, far, inner, last))

    x_rows = lax.ppermute(row_half, "col", chip_swap)
    core_rows = lax.ppermute(jnp.stack([row_half, x_rows]), "col", core_swap)
    rows = (row_half, x_rows, core_rows)

    row_term = (jnp.log(row_freq.astype(jnp.float32)) - log_total)[:, None]
    col_logs = jnp.log(col_freq[0].astype(jnp.float32))

    def pick(part, wanted):
        own, near, far, inner, last = gathered[part]
        away = wanted ^ home
        crossed = jnp.where(edge, last, inner)
        return jnp.where(
            away == 0, own, jnp.where(away == 1, near, jnp.where(away == 2, far, crossed))
        )

    def col_term(part, side):
        return jnp.stack(
            [
                lax.dynamic_slice_in_dim(
                    col_logs, chosen[s] * block + side * own_cols + part * span, span
                )[None]
                for s in range(slots)
            ]
        )

    row_grad = None
    col_sums = []
    for part in range(PARTS):
        asked = jnp.stack([pick(part, mate_chosen[s]) for s in range(slots)])
        received = lax.ppermute(asked, "row", mate_swap)
        kept = jnp.stack([pick(part, chosen[s]) for s in range(slots)])
        grads = []
        for side, cols, kind in ((half, kept, jnp.float32), (1 - half, received, jnp.bfloat16)):
            meta = jnp.stack([side * PARTS + part, col_index]).astype(jnp.int32)
            row_grad, grad = block_grads(
                meta, rows, cols, row_term, col_term(part, side), counts, row_grad, kind
            )
            grads.append(grad)
        mine, theirs = grads
        from_mate = lax.ppermute(theirs, "row", mate_swap).astype(jnp.float32)

        def block_sum(away):
            wanted = home ^ away
            total = 0.0
            for s in range(slots):
                total = total + jnp.where(chosen[s] == wanted, mine[s], 0.0)
                total = total + jnp.where(mate_chosen[s] == wanted, from_mate[s], 0.0)
            return total

        crossed = block_sum(3).astype(jnp.bfloat16)
        carried = lax.ppermute(crossed, "row", from_edge)
        inner = lax.ppermute(crossed, "row", inner_swap)
        near = lax.ppermute(block_sum(1).astype(jnp.bfloat16), "row", near_swap)
        far_sum = block_sum(2) + carried.astype(jnp.float32)
        far = lax.ppermute(far_sum.astype(jnp.bfloat16), "row", far_swap)
        col_sums.append(
            block_sum(0)
            + near.astype(jnp.float32)
            + far.astype(jnp.float32)
            + inner.astype(jnp.float32)
        )

    from_core = lax.ppermute(jnp.stack([row_grad[1], row_grad[3]]), "col", core_swap)
    away_rows = (row_grad[2] + from_core[1]).astype(jnp.bfloat16)
    from_chip = lax.ppermute(away_rows, "col", chip_swap)
    own_grad = row_grad[0] + from_core[0] + from_chip.astype(jnp.float32)
    return updates(
        row_embed, row_accum, col_embed, col_accum, row_freq, excluded, block, own_grad,
        jnp.concatenate(col_sums, axis=0),
    )


def updates(
    row_embed, row_accum, col_embed, col_accum, row_freq, excluded, block, own_grad, col_grad
):
    own_rows = row_embed.shape[0]
    col_index = lax.axis_index("col")
    row_index = lax.axis_index("row")
    own_freq = lax.dynamic_slice_in_dim(row_freq, col_index * own_rows, own_rows).astype(
        jnp.float32
    )
    row_ids = row_index * block + col_index * own_rows + jnp.arange(own_rows, dtype=jnp.int32)
    decayed = jnp.all(row_ids[:, None] != excluded[None, :], axis=1)
    freq_root = jnp.sqrt(own_freq)
    decay_coef = jnp.where(decayed, decay_rate * freq_root / (freq_root + 30.0), jnp.float32(0.0))
    full_grad = own_grad + decay_coef[:, None] * row_embed
    row_accum_new = row_accum + full_grad * full_grad
    row_embed_new = row_embed - learn_rate * full_grad / jnp.sqrt(row_accum_new)
    col_step = col_grad[None]
    col_accum_new = col_accum + col_step * col_step
    col_embed_new = col_embed - learn_rate * col_step / jnp.sqrt(col_accum_new)
    return (row_embed_new, row_accum_new, col_embed_new, col_accum_new)


def gathered_body(
    row_embed,
    row_accum,
    col_embed,
    col_accum,
    col_freq,
    row_freq,
    block_cols,
    counts,
    excluded,
    log_total,
):
    block = counts.shape[3]
    slots = counts.shape[2]
    width = row_embed.shape[1]
    chosen = block_cols[0, 0]
    block_rows = lax.all_gather(row_embed.astype(jnp.bfloat16), "col", axis=0, tiled=True)
    group = lax.all_gather(col_embed[0].astype(jnp.bfloat16), "row", axis=0, tiled=True)
    row_term = (jnp.log(row_freq.astype(jnp.float32)) - log_total)[:, None]
    col_logs = jnp.log(col_freq[0].astype(jnp.float32))
    row_grad = jnp.zeros((block, width), jnp.float32)
    summed = jnp.zeros(group.shape, jnp.float32)
    for slot in range(slots):
        start = chosen[slot] * block
        cols = lax.dynamic_slice_in_dim(group, start, block)
        predicted = lax.dot_general(
            block_rows, cols, (((1,), (1,)), ((), ())), preferred_element_type=jnp.float32
        )
        shifted = predicted + row_term + lax.dynamic_slice_in_dim(col_logs, start, block)[None]
        cell = cell_grads(counts[0, 0, slot], shifted, block)
        row_grad = row_grad + jnp.dot(cell, cols, preferred_element_type=jnp.float32)
        term = lax.dot_general(
            cell, block_rows, (((0,), (0,)), ((), ())), preferred_element_type=jnp.float32
        )
        summed = lax.dynamic_update_slice_in_dim(summed, term, start, 0)
    col_grad = lax.psum_scatter(summed, "row", scatter_dimension=0, tiled=True)
    own_grad = lax.psum_scatter(row_grad, "col", scatter_dimension=0, tiled=True)
    return updates(
        row_embed, row_accum, col_embed, col_accum, row_freq, excluded, block, own_grad, col_grad
    )


def body(row_embed, row_accum, col_embed, col_accum, col_freq, row_freq, block_cols, counts, *rest):
    halves = lax.axis_size("row") == 8 and 2 * col_embed.shape[1] == counts.shape[3]
    pick = crossed_body if halves and lax.axis_size("col") == 4 else gathered_body
    return pick(
        row_embed, row_accum, col_embed, col_accum, col_freq, row_freq, block_cols, counts, *rest
    )


def solution(mesh):
    in_specs = (
        P(("row", "col"), None),
        P(("row", "col"), None),
        P("col", "row", None),
        P("col", "row", None),
        P("col", None),
        P("row"),
        P("row", "col", None),
        P("row", "col", None, None, None),
        P(),
        P(),
    )
    out_specs = (
        P(("row", "col"), None),
        P(("row", "col"), None),
        P("col", "row", None),
        P("col", "row", None),
    )
    return jax.shard_map(body, mesh=mesh, in_specs=in_specs, out_specs=out_specs, check_vma=False)
```

```python
import functools

import jax
import jax.numpy as jnp
from jax import lax
from jax.experimental import pallas as pl
from jax.experimental.pallas import tpu as pltpu
from jax.sharding import PartitionSpec as P

learn_rate = 0.2
decay_rate = 0.5

LANES = 128
CUTS = (2, 2)

small_cost = pl.CostEstimate(flops=1, bytes_accessed=1, transcendentals=0)
whole = pl.BlockSpec(memory_space=pltpu.VMEM)
smalls = pl.BlockSpec(memory_space=pltpu.SMEM)
anywhere = pl.BlockSpec(memory_space=pl.ANY)
done_shape = pltpu.HBM((8, 128), jnp.float32)
MIB = 1024 * 1024


def cell_grads(count_block, shifted, block):
    safe_count = jnp.maximum(count_block, 1).astype(jnp.float32)
    weight = (0.1 / block) + (0.25 / block) * jnp.sqrt(safe_count)
    fitted = weight * (shifted - jnp.log(safe_count))
    hinge_grad = (0.5 / block) * jnp.tanh(0.5 * shifted) + (0.5 / block)
    return jnp.where(count_block > 0, fitted, hinge_grad).astype(jnp.bfloat16)


def in_order(
    kernel, tokens, out_shape, in_specs, out_specs=None, grid=(), vmem=16, scalars=None
):
    ahead = scalars is not None

    def wrapped(*refs):
        done = refs[-1]
        done[...] = jnp.zeros_like(done)
        kernel(*refs[:ahead], *refs[ahead + len(tokens) : -1])

    done_spec = pl.BlockSpec((8, 128), lambda *ids: (0, 0)) if grid else whole
    out_specs = [whole] * len(out_shape) if out_specs is None else out_specs
    call = pl.pallas_call(
        wrapped,
        grid_spec=pltpu.PrefetchScalarGridSpec(
            num_scalar_prefetch=int(ahead),
            grid=grid,
            in_specs=[anywhere] * len(tokens) + list(in_specs),
            out_specs=list(out_specs) + [done_spec],
        ),
        out_shape=list(out_shape) + [done_shape],
        cost_estimate=small_cost,
        compiler_params=pltpu.CompilerParams(vmem_limit_bytes=vmem * MIB),
    )
    held = [
        pltpu.with_memory_space_constraint(token, pltpu.HBM) if token.shape == (8, 128) else token
        for token in tokens
    ]
    return lambda *args: call(*([scalars] if ahead else []), *held, *args)


def in_vmem(*values):
    return [pltpu.with_memory_space_constraint(value, pltpu.VMEM) for value in values]


def in_hbm(*values):
    return [pltpu.with_memory_space_constraint(value, pltpu.HBM) for value in values]


def gated(value, *tokens):
    return pl.pallas_call(
        lambda *refs: None,
        in_specs=[anywhere] * (1 + len(tokens)),
        out_specs=anywhere,
        out_shape=jax.ShapeDtypeStruct(value.shape, value.dtype),
        input_output_aliases={0: 0},
        cost_estimate=small_cost,
        compiler_params=pltpu.CompilerParams(vmem_limit_bytes=MIB),
    )(value, *tokens)


def halve_kernel(whole_cols, half_cols):
    half_cols[...] = whole_cols[0].astype(jnp.bfloat16)


def halved(col_embed, start, units, tokens):
    width = col_embed.shape[2]
    return in_order(
        halve_kernel,
        tokens,
        [pltpu.HBM((units * LANES, width), jnp.bfloat16)],
        [pl.BlockSpec((1, LANES, width), lambda unit: (0, start + unit, 0))],
        [pl.BlockSpec((LANES, width), lambda unit: (unit, 0))],
        grid=(units,),
    )(pltpu.with_memory_space_constraint(col_embed, pltpu.HBM))


def pick_kernel(slots, seat, own, near, far, cross, asked, kept):
    for first, out in ((5, asked), (3, kept)):
        for slot in range(slots):
            for away, ref in enumerate((own, near, far, cross)):

                @pl.when(seat[first + slot] == away)
                def _(ref=ref, out=out, slot=slot):
                    for unit in range(out.shape[0]):
                        out[unit, pl.ds(slot * LANES, LANES), :] = ref[pl.ds(unit * LANES, LANES), :]


def picked(seat, pieces, slots, tokens):
    size, width = pieces[0].shape
    shape = (size // LANES, slots * LANES, width)
    return in_order(
        functools.partial(pick_kernel, slots),
        tokens,
        [jax.ShapeDtypeStruct(shape, jnp.bfloat16)] * 2,
        [smalls] + [whole] * 4,
    )(seat, *in_hbm(pieces[0]), *pieces[1:])


def count_terms(count, row_term, col_logs, block):
    safe = jnp.maximum(count, 1).astype(jnp.float32)
    some = (0.1 / block) + (0.25 / block) * jnp.sqrt(safe)
    return jnp.where(count > 0, some, 0.0), jnp.log(safe) - (row_term + col_logs)


def block_terms(rows, cols, weight, target, block):
    predicted = lax.dot_general(
        rows, cols, (((1,), (1,)), ((), ())), preferred_element_type=jnp.float32
    )
    error = predicted - target
    hinge_grad = (0.5 / block) * jnp.tanh(0.5 * error) + (0.5 / block)
    cell = jnp.where(weight > 0.0, weight * error, hinge_grad).astype(jnp.bfloat16)
    return jnp.dot(cell, cols, preferred_element_type=jnp.float32), lax.dot_general(
        cell, rows, (((0,), (0,)), ((), ())), preferred_element_type=jnp.float32
    )


def own_kernel(start, slots, seat, row_term, col_freq, own, core, chip, both, cols, *rest):
    counts, rest = rest[: 2 * slots], rest[2 * slots :]
    home_grad, core_grad, col_grad, weight, target = rest
    step = pl.program_id(0)
    block, size = row_term.shape[0], own.shape[0]

    @pl.when(step == 0)
    def _():
        home_grad[...] = jnp.zeros_like(home_grad)
        core_grad[...] = jnp.zeros_like(core_grad)

    def logs(slot, which):
        at = seat[1 + slot] * block + (seat[0] ^ which) * (block // 2) + (start + step) * LANES
        return jnp.log(col_freq[:, pl.ds(pl.multiple_of(at, LANES), LANES)].astype(jnp.float32))

    col_logs = [[logs(slot, which) for slot in range(slots)] for which in range(2)]
    some = cols[0]
    total = None
    for piece, ref in enumerate((own, core, chip, both)):
        at = pl.ds(pl.multiple_of((seat[7] ^ piece) * size, size), size)
        sides = []
        for which in range(2):
            pairs = [
                count_terms(
                    counts[which * slots + slot][0, 0, 0, at, :],
                    row_term[at, :],
                    col_logs[which][slot],
                    block,
                )
                for slot in range(slots)
            ]
            sides.append([jnp.concatenate(pair, axis=1) for pair in zip(*pairs)])
        row_part, col_part = block_terms(ref[...], some, *sides[0], block)
        row_grad = core_grad if piece % 2 else home_grad
        row_grad[piece // 2] += row_part
        total = col_part if total is None else total + col_part
        weight[step, at, :], target[step, at, :] = sides[1]
    col_grad[0] = total


def other_kernel(block, seat, own, core, chip, both, cols, weight, target, *rest):
    home_before, core_before, home_grad, core_grad, col_grad = rest
    size = own.shape[0]
    for unit in range(cols.shape[0]):
        total = None
        for piece, ref in enumerate((own, core, chip, both)):
            at = pl.ds(pl.multiple_of((seat[7] ^ piece) * size, size), size)
            row_part, col_part = block_terms(
                ref[...], cols[unit], weight[unit, at, :], target[unit, at, :], block
            )
            row_grad = core_grad if piece % 2 else home_grad
            before = row_grad if unit else (core_before if piece % 2 else home_before)
            row_grad[piece // 2] = before[piece // 2] + row_part
            total = col_part if total is None else total + col_part
        col_grad[unit] = total.astype(col_grad.dtype)


def own_grads(seat, row_term, col_freq, rows, cols, counts, start, tokens):
    size, width = rows[0].shape
    units, both, _ = cols.shape
    slots, block = counts.shape[2:4]
    halves = block // 2 // LANES
    grad_shape = pltpu.VMEM((2, size, width), jnp.float32)
    term_shape = pltpu.VMEM((units, block, both), jnp.float32)
    col_spec = pl.BlockSpec((1, both, width), lambda unit, seat: (unit, 0, 0))

    def count_spec(slot, which):
        return pl.BlockSpec(
            (1, 1, 1, block, LANES),
            lambda unit, seat: (0, 0, slot, 0, (seat[0] ^ which) * halves + start + unit),
        )

    count_specs = [count_spec(slot, which) for which in range(2) for slot in range(slots)]
    counts = pltpu.with_memory_space_constraint(counts, pltpu.HBM)
    return in_order(
        functools.partial(own_kernel, start, slots),
        tokens,
        [grad_shape, grad_shape, pltpu.HBM(cols.shape, jnp.float32), term_shape, term_shape],
        [whole] * 6 + [col_spec] + count_specs,
        [whole, whole, col_spec, whole, whole],
        grid=(units,),
        vmem=32,
        scalars=seat,
    )(row_term, col_freq, *rows, cols, *[counts] * (2 * slots))


def other_grads(seat, rows, cols, weight, target, before, tokens):
    size, width = rows[0].shape
    grad_shape = jax.ShapeDtypeStruct((2, size, width), jnp.float32)
    return in_order(
        functools.partial(other_kernel, weight.shape[1]),
        tokens,
        [grad_shape, grad_shape, pltpu.HBM(cols.shape, jnp.bfloat16)],
        [smalls] + [whole] * 9,
        vmem=24,
    )(seat, *rows, cols, *in_vmem(weight, target, *before))


def sum_kernel(slots, seat, mine, theirs, home, near, far, cross):
    for unit in range(mine.shape[0]):
        for away, out in enumerate((home, near, far, cross)):
            total = jnp.zeros(out.shape[1:], jnp.float32)
            for slot in range(slots):
                at = pl.ds(slot * LANES, LANES)
                total = total + jnp.where(seat[3 + slot] == away, mine[unit, at, :], 0.0)
                total = total + jnp.where(
                    seat[5 + slot] == away, theirs[unit, at, :].astype(jnp.float32), 0.0
                )
            out[unit] = total.astype(out.dtype)


def block_sums(seat, mine, theirs, slots, tokens):
    units, _, width = mine.shape
    shape = (units, LANES, width)
    return in_order(
        functools.partial(sum_kernel, slots),
        tokens,
        [
            pltpu.HBM(shape, jnp.float32),
            pltpu.HBM(shape, jnp.bfloat16),
            jax.ShapeDtypeStruct(shape, jnp.float32),
            jax.ShapeDtypeStruct(shape, jnp.bfloat16),
        ],
        [smalls, whole, whole],
    )(seat, mine, theirs)


def crossed_body(
    row_embed,
    row_accum,
    col_embed,
    col_accum,
    col_freq,
    row_freq,
    block_cols,
    counts,
    excluded,
    log_total,
):
    block = counts.shape[3]
    slots = counts.shape[2]
    width = col_embed.shape[2]
    row_index = lax.axis_index("row")
    col_index = lax.axis_index("col")
    half = row_index % 2
    home = row_index // 2

    mate_swap = [(i, i ^ 1) for i in range(8)]
    near_swap = [(i, i ^ 2) for i in range(8)]
    far_swap = [(i, i ^ 4) for i in range(8)]
    core_swap = [(i, i ^ 1) for i in range(4)]
    chip_swap = [(i, i ^ 2) for i in range(4)]

    def swap(name, value, axis, pairs):
        with jax.named_scope(name):
            return lax.ppermute(value, axis, pairs)

    chosen = block_cols[0, 0]
    mate_chosen = swap("mate_chosen", chosen, "row", mate_swap)
    seat = jnp.concatenate(
        [half[None], chosen, chosen ^ home, mate_chosen ^ home, col_index[None]]
    ).astype(jnp.int32)

    starts = [sum(CUTS[:part]) for part in range(len(CUTS))]

    def spread_cols(part, *tokens):
        own, done = halved(col_embed, starts[part], CUTS[part], tokens)
        far = swap(f"cols_far_{part}", own, "row", far_swap)
        near = swap(f"cols_near_{part}", own, "row", near_swap)
        return (own, near, far), done

    def all_cols(part, own, near, far):
        return own, near, far, swap(f"cols_cross_{part}", far, "row", near_swap)

    cols_0, done = spread_cols(0)
    row_half = row_embed.astype(jnp.bfloat16)
    core_rows = swap("core_rows", row_half, "col", core_swap)
    chip_rows = swap("chip_rows", row_half, "col", chip_swap)
    both_rows = swap("both_rows", chip_rows, "col", core_swap)
    rows = (row_half, core_rows, chip_rows, both_rows)
    row_term = (jnp.log(row_freq.astype(jnp.float32)) - log_total)[:, None]

    def own(part, cols, done):
        home_grad, core_grad, col_grad, *terms, done = own_grads(
            seat, row_term, col_freq, rows, cols, counts, starts[part], (done,)
        )
        return (home_grad, core_grad), col_grad, terms, done

    def other(cols, terms, before, *tokens):
        home_grad, core_grad, col_grad, done = other_grads(
            seat, rows, cols, *terms, before, tokens
        )
        return (home_grad, core_grad), col_grad, done

    parts = len(CUTS)
    cols, row_grads, summed, sent = all_cols(0, *cols_0), [], [], ()

    def sum_part(part, mine, from_mate, *tokens):
        home_sum, near, far, cross, done = block_sums(seat, mine, from_mate, slots, tokens)
        cross = swap(f"grads_cross_{part}", cross, "row", near_swap)
        return (home_sum, near, far, cross), done

    def send_part(part, sums):
        home_sum, near, far, cross = sums
        far = (far + cross.astype(jnp.float32)).astype(jnp.bfloat16)
        near = swap(f"grads_near_{part}", near, "row", near_swap)
        far = swap(f"grads_far_{part}", far, "row", far_swap)
        total = home_sum + near.astype(jnp.float32) + far.astype(jnp.float32)
        summed.append(total.reshape(-1, width))
        return near, far

    for part in range(parts):
        asked, kept, done = picked(seat, cols, slots, (done, both_rows))
        received = swap(f"cols_mate_{part}", asked, "row", mate_swap)
        if part + 1 < parts:
            cols, done = spread_cols(part + 1, done)
        own_rows, mine, terms, done = own(part, kept, done)
        if part + 1 < parts:
            own_cols, near, far = cols
            cols = all_cols(part + 1, own_cols, near, gated(far, done, near))
        if part:
            sums, done = sum_part(part - 1, *waiting, done, *sent)
            sent = send_part(part - 1, sums)
            other_rows, theirs, done = other(received, terms, own_rows, done, sums[3])
        else:
            other_rows, theirs, done = other(received, terms, own_rows, done)
        row_grads.append(other_rows)
        waiting = mine, swap(f"grads_mate_{part}", theirs, "row", mate_swap)

    home_grad, core_grad = [sum(pieces[1:], pieces[0]) for pieces in zip(*row_grads)]
    from_core = swap("row_grads_core", core_grad, "col", core_swap)
    chip_grad = (home_grad[1] + from_core[1]).astype(jnp.bfloat16)
    from_chip = swap("row_grads_chip", chip_grad, "col", chip_swap)
    own_grad = home_grad[0] + from_core[0] + from_chip.astype(jnp.float32)
    row_new = row_updates(row_embed, row_accum, row_freq, excluded, block, own_grad)

    sums, done = sum_part(parts - 1, *waiting, done, *sent)
    send_part(parts - 1, sums)
    return (*row_new, *col_updates(col_embed, col_accum, jnp.concatenate(summed, axis=0)))


def row_updates(row_embed, row_accum, row_freq, excluded, block, own_grad):
    own_rows = row_embed.shape[0]
    col_index = lax.axis_index("col")
    row_index = lax.axis_index("row")
    own_freq = lax.dynamic_slice_in_dim(row_freq, col_index * own_rows, own_rows).astype(
        jnp.float32
    )
    row_ids = row_index * block + col_index * own_rows + jnp.arange(own_rows, dtype=jnp.int32)
    decayed = jnp.all(row_ids[:, None] != excluded[None, :], axis=1)
    freq_root = jnp.sqrt(own_freq)
    decay_coef = jnp.where(decayed, decay_rate * freq_root / (freq_root + 30.0), jnp.float32(0.0))
    full_grad = own_grad + decay_coef[:, None] * row_embed
    row_accum_new = row_accum + full_grad * full_grad
    row_embed_new = row_embed - learn_rate * full_grad / jnp.sqrt(row_accum_new)
    return row_embed_new, row_accum_new


def col_updates(col_embed, col_accum, col_grad):
    col_step = col_grad[None]
    col_accum_new = col_accum + col_step * col_step
    col_embed_new = col_embed - learn_rate * col_step / jnp.sqrt(col_accum_new)
    return col_embed_new, col_accum_new


def gathered_body(
    row_embed,
    row_accum,
    col_embed,
    col_accum,
    col_freq,
    row_freq,
    block_cols,
    counts,
    excluded,
    log_total,
):
    block = counts.shape[3]
    slots = counts.shape[2]
    width = row_embed.shape[1]
    chosen = block_cols[0, 0]
    block_rows = lax.all_gather(row_embed.astype(jnp.bfloat16), "col", axis=0, tiled=True)
    group = lax.all_gather(col_embed[0].astype(jnp.bfloat16), "row", axis=0, tiled=True)
    row_term = (jnp.log(row_freq.astype(jnp.float32)) - log_total)[:, None]
    col_logs = jnp.log(col_freq[0].astype(jnp.float32))
    row_grad = jnp.zeros((block, width), jnp.float32)
    summed = jnp.zeros(group.shape, jnp.float32)
    for slot in range(slots):
        start = chosen[slot] * block
        cols = lax.dynamic_slice_in_dim(group, start, block)
        predicted = lax.dot_general(
            block_rows, cols, (((1,), (1,)), ((), ())), preferred_element_type=jnp.float32
        )
        shifted = predicted + row_term + lax.dynamic_slice_in_dim(col_logs, start, block)[None]
        cell = cell_grads(counts[0, 0, slot], shifted, block)
        row_grad = row_grad + jnp.dot(cell, cols, preferred_element_type=jnp.float32)
        term = lax.dot_general(
            cell, block_rows, (((0,), (0,)), ((), ())), preferred_element_type=jnp.float32
        )
        summed = lax.dynamic_update_slice_in_dim(summed, term, start, 0)
    col_grad = lax.psum_scatter(summed, "row", scatter_dimension=0, tiled=True)
    own_grad = lax.psum_scatter(row_grad, "col", scatter_dimension=0, tiled=True)
    return (
        *row_updates(row_embed, row_accum, row_freq, excluded, block, own_grad),
        *col_updates(col_embed, col_accum, col_grad),
    )


def body(row_embed, row_accum, col_embed, col_accum, col_freq, row_freq, block_cols, counts, *rest):
    halves = lax.axis_size("row") == 8 and 2 * col_embed.shape[1] == counts.shape[3]
    pick = crossed_body if halves and lax.axis_size("col") == 4 else gathered_body
    return pick(
        row_embed, row_accum, col_embed, col_accum, col_freq, row_freq, block_cols, counts, *rest
    )


def solution(mesh):
    in_specs = (
        P(("row", "col"), None),
        P(("row", "col"), None),
        P("col", "row", None),
        P("col", "row", None),
        P("col", None),
        P("row"),
        P("row", "col", None),
        P("row", "col", None, None, None),
        P(),
        P(),
    )
    out_specs = (
        P(("row", "col"), None),
        P(("row", "col"), None),
        P("col", "row", None),
        P("col", "row", None),
    )
    return jax.shard_map(body, mesh=mesh, in_specs=in_specs, out_specs=out_specs, check_vma=False)
```

```python
import functools

import jax
import jax.numpy as jnp
from jax import lax
from jax.experimental import pallas as pl
from jax.experimental.pallas import tpu as pltpu
from jax.sharding import PartitionSpec as P

learn_rate = 0.2
decay_rate = 0.5

LANES = 128
CUTS = (2, 2)

small_cost = pl.CostEstimate(flops=1, bytes_accessed=1, transcendentals=0)
whole = pl.BlockSpec(memory_space=pltpu.VMEM)
smalls = pl.BlockSpec(memory_space=pltpu.SMEM)
anywhere = pl.BlockSpec(memory_space=pl.ANY)
done_shape = pltpu.HBM((8, 128), jnp.float32)
MIB = 1024 * 1024


def cell_grads(count_block, shifted, block):
    safe_count = jnp.maximum(count_block, 1).astype(jnp.float32)
    weight = (0.1 / block) + (0.25 / block) * jnp.sqrt(safe_count)
    fitted = weight * (shifted - jnp.log(safe_count))
    hinge_grad = (0.5 / block) * jnp.tanh(0.5 * shifted) + (0.5 / block)
    return jnp.where(count_block > 0, fitted, hinge_grad).astype(jnp.bfloat16)


def in_order(
    kernel, tokens, out_shape, in_specs, out_specs=None, grid=(), vmem=16, scalars=None, aliases={}
):
    ahead = scalars is not None

    def wrapped(*refs):
        done = refs[-1]
        done[...] = jnp.zeros_like(done)
        kernel(*refs[:ahead], *refs[ahead + len(tokens) : -1])

    done_spec = pl.BlockSpec((8, 128), lambda *ids: (0, 0)) if grid else whole
    out_specs = [whole] * len(out_shape) if out_specs is None else out_specs
    call = pl.pallas_call(
        wrapped,
        grid_spec=pltpu.PrefetchScalarGridSpec(
            num_scalar_prefetch=int(ahead),
            grid=grid,
            in_specs=[anywhere] * len(tokens) + list(in_specs),
            out_specs=list(out_specs) + [done_spec],
        ),
        out_shape=list(out_shape) + [done_shape],
        input_output_aliases=aliases,
        cost_estimate=small_cost,
        compiler_params=pltpu.CompilerParams(vmem_limit_bytes=vmem * MIB),
    )
    return lambda *args: call(*([scalars] if ahead else []), *held(tokens), *args)


def held(tokens):
    return [*map(lambda token: in_hbm(token)[0] if token.shape == (8, 128) else token, tokens)]


def in_vmem(*values):
    return [pltpu.with_memory_space_constraint(value, pltpu.VMEM) for value in values]


def in_hbm(*values):
    return [pltpu.with_memory_space_constraint(value, pltpu.HBM) for value in values]


def gated(values, tokens):
    return pl.pallas_call(
        lambda *refs: None,
        in_specs=[anywhere] * (len(values) + len(tokens)),
        out_specs=[anywhere] * len(values),
        out_shape=[jax.ShapeDtypeStruct(value.shape, value.dtype) for value in values],
        input_output_aliases={i: i for i in range(len(values))},
        cost_estimate=small_cost,
        compiler_params=pltpu.CompilerParams(vmem_limit_bytes=MIB),
    )(*values, *held(tokens))


def halve_kernel(whole_values, half_values):
    half_values[...] = whole_values[...].reshape(half_values.shape).astype(half_values.dtype)


def halved(values, start, rows, tokens):
    lead, width = values.shape[:-2], values.shape[-1]
    return in_order(
        halve_kernel,
        tokens,
        [jax.ShapeDtypeStruct((rows, width), jnp.bfloat16)],
        [
            pl.BlockSpec(
                (*lead, LANES, width),
                lambda step: (*[0] * len(lead), start // LANES + step, 0),
            )
        ],
        [pl.BlockSpec((LANES, width), lambda step: (step, 0))],
        grid=(rows // LANES,),
        vmem=4,
    )(*in_hbm(values))


def pick_kernel(slots, seat, own, near, far, cross, asked, kept):
    for first, out in ((5, asked), (3, kept)):
        for slot in range(slots):
            for away, ref in enumerate((own, near, far, cross)):

                @pl.when(seat[first + slot] == away)
                def _(ref=ref, out=out, slot=slot):
                    for unit in range(out.shape[0]):
                        out[unit, pl.ds(slot * LANES, LANES), :] = ref[pl.ds(unit * LANES, LANES), :]


def picked(seat, pieces, slots, tokens):
    size, width = pieces[0].shape
    shape = (size // LANES, slots * LANES, width)
    return in_order(
        functools.partial(pick_kernel, slots),
        tokens,
        [jax.ShapeDtypeStruct(shape, jnp.bfloat16)] * 2,
        [smalls] + [whole] * 4,
    )(seat, *in_hbm(pieces[0]), *pieces[1:])


def count_terms(count, row_term, col_logs, block):
    safe = jnp.maximum(count, 1).astype(jnp.float32)
    some = (0.1 / block) + (0.25 / block) * jnp.sqrt(safe)
    return jnp.where(count > 0, some, 0.0), jnp.log(safe) - (row_term + col_logs)


def block_terms(rows, cols, weight, target, block):
    predicted = lax.dot_general(
        rows, cols, (((1,), (1,)), ((), ())), preferred_element_type=jnp.float32
    )
    error = predicted - target
    hinge_grad = (0.5 / block) * jnp.tanh(0.5 * error) + (0.5 / block)
    cell = jnp.where(weight > 0.0, weight * error, hinge_grad).astype(jnp.bfloat16)
    return jnp.dot(cell, cols, preferred_element_type=jnp.float32), lax.dot_general(
        cell, rows, (((0,), (0,)), ((), ())), preferred_element_type=jnp.float32
    )


def own_kernel(start, slots, seat, row_term, col_freq, own, core, chip, both, cols, *rest):
    counts, rest = rest[: 2 * slots], rest[2 * slots :]
    row_grads, (col_grad, weight, target) = rest[:4], rest[4:]
    step = pl.program_id(0)
    block, size = row_term.shape[0], own.shape[0]

    @pl.when(step == 0)
    def _():
        for row_grad in row_grads:
            row_grad[...] = jnp.zeros_like(row_grad)

    def logs(slot, which):
        at = seat[1 + slot] * block + (seat[0] ^ which) * (block // 2) + (start + step) * LANES
        return jnp.log(col_freq[:, pl.ds(pl.multiple_of(at, LANES), LANES)].astype(jnp.float32))

    col_logs = [[logs(slot, which) for slot in range(slots)] for which in range(2)]
    some = cols[0]
    total = None
    for piece, ref in enumerate((own, core, chip, both)):
        at = pl.ds(pl.multiple_of((seat[7] ^ piece) * size, size), size)
        sides = []
        for which in range(2):
            pairs = [
                count_terms(
                    counts[which * slots + slot][0, 0, 0, at, :],
                    row_term[at, :],
                    col_logs[which][slot],
                    block,
                )
                for slot in range(slots)
            ]
            sides.append([jnp.concatenate(pair, axis=1) for pair in zip(*pairs)])
        row_part, col_part = block_terms(ref[...], some, *sides[0], block)
        row_grads[piece][...] += row_part
        total = col_part if total is None else total + col_part
        weight[step, at, :], target[step, at, :] = sides[1]
    col_grad[0] = total


def other_kernel(block, earlier, seat, own, core, chip, both, cols, weight, target, *rest):
    grads, sums = rest[: 4 + 4 * earlier], rest[4 + 4 * earlier : -1]
    col_grad = rest[-1]
    size = own.shape[0]
    for unit in range(cols.shape[0]):
        total = None
        for piece, ref in enumerate((own, core, chip, both)):
            at = pl.ds(pl.multiple_of((seat[7] ^ piece) * size, size), size)
            row_part, col_part = block_terms(
                ref[...], cols[unit], weight[unit, at, :], target[unit, at, :], block
            )
            for before in [sums[piece]] if unit else grads[piece::4]:
                row_part = row_part + before[...]
            sums[piece][...] = row_part
            total = col_part if total is None else total + col_part
        col_grad[unit] = total.astype(col_grad.dtype)


def own_grads(seat, row_term, col_freq, rows, cols, counts, start, tokens):
    size, width = rows[0].shape
    units, both, _ = cols.shape
    slots, block = counts.shape[2:4]
    halves = block // 2 // LANES
    grad_shape = pltpu.VMEM((size, width), jnp.float32)
    term_shape = pltpu.VMEM((units, block, both), jnp.float32)
    col_spec = pl.BlockSpec((1, both, width), lambda unit, seat: (unit, 0, 0))

    def count_spec(slot, which):
        return pl.BlockSpec(
            (1, 1, 1, block, LANES),
            lambda unit, seat: (0, 0, slot, 0, (seat[0] ^ which) * halves + start + unit),
        )

    count_specs = [count_spec(slot, which) for which in range(2) for slot in range(slots)]
    counts = pltpu.with_memory_space_constraint(counts, pltpu.HBM)
    return in_order(
        functools.partial(own_kernel, start, slots),
        tokens,
        [grad_shape] * 4 + [pltpu.HBM(cols.shape, jnp.float32), term_shape, term_shape],
        [whole] * 6 + [col_spec] + count_specs,
        [whole] * 4 + [col_spec, whole, whole],
        grid=(units,),
        vmem=32,
        scalars=seat,
    )(row_term, col_freq, *rows, cols, *[counts] * (2 * slots))


def other_grads(seat, rows, cols, weight, target, before, earlier, tokens):
    size, width = rows[0].shape
    grad_shape = jax.ShapeDtypeStruct((size, width), jnp.float32)
    return in_order(
        functools.partial(other_kernel, weight.shape[1], len(earlier)),
        tokens,
        [grad_shape] * 4 + [pltpu.HBM(cols.shape, jnp.bfloat16)],
        [smalls] + [whole] * (11 + 4 * len(earlier)),
        vmem=32,
    )(
        seat,
        *rows,
        cols,
        *in_vmem(weight, target, *before),
        *[grad for grads in earlier for grad in grads],
    )


def sum_kernel(slots, seat, mine, theirs, home, near, far, cross):
    for unit in range(mine.shape[0]):
        for away, out in enumerate((home, near, far, cross)):
            total = jnp.zeros(out.shape[1:], jnp.float32)
            for slot in range(slots):
                at = pl.ds(slot * LANES, LANES)
                total = total + jnp.where(seat[3 + slot] == away, mine[unit, at, :], 0.0)
                total = total + jnp.where(
                    seat[5 + slot] == away, theirs[unit, at, :].astype(jnp.float32), 0.0
                )
            out[unit] = total.astype(out.dtype)


def block_sums(seat, mine, theirs, slots, tokens):
    units, _, width = mine.shape
    shape = (units, LANES, width)
    return in_order(
        functools.partial(sum_kernel, slots),
        tokens,
        [
            pltpu.HBM(shape, jnp.float32),
            pltpu.HBM(shape, jnp.bfloat16),
            jax.ShapeDtypeStruct(shape, jnp.float32),
            jax.ShapeDtypeStruct(shape, jnp.bfloat16),
        ],
        [smalls, whole, whole],
    )(seat, mine, theirs)


def relay_kernel(near, far, cross, near_out, far_out):
    near_out[...] = near[...]
    far_out[...] = (far[...] + cross[...].astype(jnp.float32)).astype(far_out.dtype)


def relayed(near, far, cross, tokens):
    shape = jax.ShapeDtypeStruct(far.shape, jnp.bfloat16)
    return in_order(relay_kernel, tokens, [shape] * 2, [whole] * 3, vmem=4)(near, far, cross)


def add_kernel(left, right, out):
    out[...] = (left[...] + right[...]).astype(out.dtype)


def added(left, right, tokens):
    shape = jax.ShapeDtypeStruct(left.shape, jnp.bfloat16)
    return in_order(add_kernel, tokens, [shape], [whole] * 2, vmem=4)(left, right)


def update_kernel(embed, accum, home, near, far, *rest):
    embed_new, accum_new = rest[-2:]
    grad = home[...] + near[...].astype(jnp.float32) + far[...].astype(jnp.float32)
    total = accum[...] + grad * grad
    accum_new[...] = total
    embed_new[...] = embed[...] - learn_rate * grad / jnp.sqrt(total)


def updated(embed, accum, start, sums, before, tokens):
    units, _, width = sums[0].shape
    shape = jax.ShapeDtypeStruct(embed.shape, jnp.float32)
    outer = pl.BlockSpec((1, LANES, width), lambda unit: (0, start + unit, 0))
    inner = pl.BlockSpec((1, LANES, width), lambda unit: (unit, 0, 0))
    count = len(tokens) + 5
    return in_order(
        update_kernel,
        tokens,
        [shape, shape],
        [outer, outer, inner, inner, inner] + [anywhere] * len(before),
        [outer, outer],
        grid=(units,),
        vmem=8,
        aliases={count + i: i for i in range(len(before))},
    )(*in_hbm(embed, accum), *sums, *before)


def crossed_body(
    row_embed,
    row_accum,
    col_embed,
    col_accum,
    col_freq,
    row_freq,
    block_cols,
    counts,
    excluded,
    log_total,
):
    block = counts.shape[3]
    slots = counts.shape[2]
    width = col_embed.shape[2]
    row_index = lax.axis_index("row")
    col_index = lax.axis_index("col")
    half = row_index % 2
    home = row_index // 2

    mate_swap = [(i, i ^ 1) for i in range(8)]
    near_swap = [(i, i ^ 2) for i in range(8)]
    far_swap = [(i, i ^ 4) for i in range(8)]
    core_swap = [(i, i ^ 1) for i in range(4)]
    chip_swap = [(i, i ^ 2) for i in range(4)]

    def swap(name, value, axis, pairs):
        with jax.named_scope(name):
            return lax.ppermute(value, axis, pairs)

    chosen = block_cols[0, 0]
    mate_chosen = swap("mate_chosen", chosen, "row", mate_swap)
    seat = jnp.concatenate(
        [half[None], chosen, chosen ^ home, mate_chosen ^ home, col_index[None]]
    ).astype(jnp.int32)

    starts = [sum(CUTS[:part]) for part in range(len(CUTS))]

    def far_cols(part, own):
        return own, swap(f"cols_far_{part}", own, "row", far_swap)

    def near_cols(part, own, far):
        near = swap(f"cols_near_{part}", own, "row", near_swap)
        return own, near, far, swap(f"cols_cross_{part}", far, "row", near_swap)

    cols = near_cols(0, *far_cols(0, col_embed[0, : CUTS[0] * LANES].astype(jnp.bfloat16)))
    row_half, done = halved(row_embed, 0, row_embed.shape[0], cols[:1])
    core_rows = swap("core_rows", row_half, "col", core_swap)
    chip_rows = swap("chip_rows", row_half, "col", chip_swap)
    both_rows = swap("both_rows", chip_rows, "col", core_swap)
    rows = (row_half, core_rows, chip_rows, both_rows)
    parts = len(CUTS)

    def own_cols(part, *tokens):
        if part >= parts:
            return None, tokens[0]
        return halved(col_embed, starts[part] * LANES, CUTS[part] * LANES, tokens)

    own_next, done = own_cols(1, done)
    coming = far_cols(1, *gated((own_next,), (*cols[1:3], done)))
    row_term = (jnp.log(row_freq.astype(jnp.float32)) - log_total)[:, None]

    def own(part, cols, done):
        *grads, col_grad, weight, target, done = own_grads(
            seat, row_term, col_freq, rows, cols, counts, starts[part], (done,)
        )
        return grads, col_grad, (weight, target), done

    def other(cols, terms, before, earlier, done):
        *grads, col_grad, done = other_grads(seat, rows, cols, *terms, before, earlier, (done,))
        return grads, col_grad, done

    row_grads, col_new, sent = [], (), None

    def pick_part(part, cols, coming, *tokens):
        if coming is not None:
            tokens += coming[1:]
        asked, kept, done = picked(seat, cols, slots, tokens)
        received = swap(f"cols_mate_{part}", asked, "row", mate_swap)
        after_next = None
        if coming is not None:
            cols = near_cols(part + 1, *gated(coming, (done,)))
            own_next, done = own_cols(part + 2, done)
            if own_next is not None:
                after_next = far_cols(part + 2, own_next)
        return kept, received, cols, after_next, done

    def sum_part(part, mine, from_mate, *tokens):
        home_sum, near, far, cross, done = block_sums(seat, mine, from_mate, slots, tokens)
        cross = swap(f"grads_cross_{part}", cross, "row", near_swap)
        return (home_sum, near, far, cross), done

    def send_part(part, sums, *tokens):
        home_sum, near, far, cross = sums
        near, far, done = relayed(near, far, cross, tokens)
        near = swap(f"grads_near_{part}", near, "row", near_swap)
        far = swap(f"grads_far_{part}", far, "row", far_swap)
        return (home_sum, near, far), done

    def update_part(part, sums, *tokens):
        *new, done = updated(col_embed, col_accum, starts[part], sums, col_new, tokens)
        return new, done

    *_, cross = cols
    cols = (*cols[:3], *gated((cross,), (done,)))
    kept, received, cols, coming, done = pick_part(0, cols, coming, done, core_rows, both_rows)
    for part in range(parts):
        own_rows, mine, terms, done = own(part, kept, done)
        if part + 1 < parts:
            kept, received_next, cols, coming, done = pick_part(
                part + 1, cols, coming, done, received
            )
        earlier = row_grads if part + 1 == parts else []
        other_rows, theirs, done = other(received, terms, own_rows, earlier, done)
        from_mate = swap(f"grads_mate_{part}", theirs, "row", mate_swap)
        if part:
            if sent:
                col_new, done = update_part(part - 2, sent, done)
            sums, done = sum_part(part - 1, *waiting, done)
            if part + 1 == parts:
                home_grad, core_grad, chip_grad, both_grad = other_rows
                both_core = swap("row_grads_both", both_grad, "col", core_swap)
                from_core = swap("row_grads_core", core_grad, "col", core_swap)
                chip_sum, done = added(chip_grad, both_core, (done,))
                from_chip = swap("row_grads_chip", chip_sum, "col", chip_swap)
                own_grad = home_grad + from_core + from_chip.astype(jnp.float32)
                row_new = row_updates(
                    row_embed, row_accum, row_freq, excluded, block, own_grad
                )
            sent, done = send_part(part - 1, sums, done)
        row_grads.append(other_rows)
        waiting = mine, from_mate
        received = received_next

    sums, done = sum_part(parts - 1, *waiting, done)


    *sums, cross = sums
    passed = gated(sent[:1], (*sent[1:], done)) if sent else ()
    last, done = send_part(parts - 1, (*sums, cross), done, *passed, row_new[1])
    if sent:
        col_new, done = update_part(parts - 2, (*passed, *sent[1:]), done)
    col_new, done = update_part(parts - 1, last, done)
    return (*row_new, *col_new)


def row_updates(row_embed, row_accum, row_freq, excluded, block, own_grad):
    own_rows = row_embed.shape[0]
    col_index = lax.axis_index("col")
    row_index = lax.axis_index("row")
    own_freq = lax.dynamic_slice_in_dim(row_freq, col_index * own_rows, own_rows).astype(
        jnp.float32
    )
    row_ids = row_index * block + col_index * own_rows + jnp.arange(own_rows, dtype=jnp.int32)
    decayed = jnp.all(row_ids[:, None] != excluded[None, :], axis=1)
    freq_root = jnp.sqrt(own_freq)
    decay_coef = jnp.where(decayed, decay_rate * freq_root / (freq_root + 30.0), jnp.float32(0.0))
    full_grad = own_grad + decay_coef[:, None] * row_embed
    row_accum_new = row_accum + full_grad * full_grad
    row_embed_new = row_embed - learn_rate * full_grad / jnp.sqrt(row_accum_new)
    return row_embed_new, row_accum_new


def col_updates(col_embed, col_accum, col_grad):
    col_step = col_grad[None]
    col_accum_new = col_accum + col_step * col_step
    col_embed_new = col_embed - learn_rate * col_step / jnp.sqrt(col_accum_new)
    return col_embed_new, col_accum_new


def gathered_body(
    row_embed,
    row_accum,
    col_embed,
    col_accum,
    col_freq,
    row_freq,
    block_cols,
    counts,
    excluded,
    log_total,
):
    block = counts.shape[3]
    slots = counts.shape[2]
    width = row_embed.shape[1]
    chosen = block_cols[0, 0]
    block_rows = lax.all_gather(row_embed.astype(jnp.bfloat16), "col", axis=0, tiled=True)
    group = lax.all_gather(col_embed[0].astype(jnp.bfloat16), "row", axis=0, tiled=True)
    row_term = (jnp.log(row_freq.astype(jnp.float32)) - log_total)[:, None]
    col_logs = jnp.log(col_freq[0].astype(jnp.float32))
    row_grad = jnp.zeros((block, width), jnp.float32)
    summed = jnp.zeros(group.shape, jnp.float32)
    for slot in range(slots):
        start = chosen[slot] * block
        cols = lax.dynamic_slice_in_dim(group, start, block)
        predicted = lax.dot_general(
            block_rows, cols, (((1,), (1,)), ((), ())), preferred_element_type=jnp.float32
        )
        shifted = predicted + row_term + lax.dynamic_slice_in_dim(col_logs, start, block)[None]
        cell = cell_grads(counts[0, 0, slot], shifted, block)
        row_grad = row_grad + jnp.dot(cell, cols, preferred_element_type=jnp.float32)
        term = lax.dot_general(
            cell, block_rows, (((0,), (0,)), ((), ())), preferred_element_type=jnp.float32
        )
        summed = lax.dynamic_update_slice_in_dim(summed, term, start, 0)
    col_grad = lax.psum_scatter(summed, "row", scatter_dimension=0, tiled=True)
    own_grad = lax.psum_scatter(row_grad, "col", scatter_dimension=0, tiled=True)
    return (
        *row_updates(row_embed, row_accum, row_freq, excluded, block, own_grad),
        *col_updates(col_embed, col_accum, col_grad),
    )


def body(row_embed, row_accum, col_embed, col_accum, col_freq, row_freq, block_cols, counts, *rest):
    halves = lax.axis_size("row") == 8 and 2 * col_embed.shape[1] == counts.shape[3]
    pick = crossed_body if halves and lax.axis_size("col") == 4 else gathered_body
    return pick(
        row_embed, row_accum, col_embed, col_accum, col_freq, row_freq, block_cols, counts, *rest
    )


def solution(mesh):
    in_specs = (
        P(("row", "col"), None),
        P(("row", "col"), None),
        P("col", "row", None),
        P("col", "row", None),
        P("col", None),
        P("row"),
        P("row", "col", None),
        P("row", "col", None, None, None),
        P(),
        P(),
    )
    out_specs = (
        P(("row", "col"), None),
        P(("row", "col"), None),
        P("col", "row", None),
        P("col", "row", None),
    )
    return jax.shard_map(body, mesh=mesh, in_specs=in_specs, out_specs=out_specs, check_vma=False)
```

```python
import functools

import jax
import jax.numpy as jnp
from jax import lax
from jax.experimental import pallas as pl
from jax.experimental.pallas import tpu as pltpu
from jax.sharding import PartitionSpec as P

learn_rate = 0.2
decay_rate = 0.5

LANES = 128
CUTS = (2, 2)

small_cost = pl.CostEstimate(flops=1, bytes_accessed=1, transcendentals=0)
whole = pl.BlockSpec(memory_space=pltpu.VMEM)
smalls = pl.BlockSpec(memory_space=pltpu.SMEM)
anywhere = pl.BlockSpec(memory_space=pl.ANY)
done_shape = pltpu.HBM((8, 128), jnp.float32)
MIB = 1024 * 1024


def cell_grads(count_block, shifted, block):
    safe_count = jnp.maximum(count_block, 1).astype(jnp.float32)
    weight = (0.1 / block) + (0.25 / block) * jnp.sqrt(safe_count)
    fitted = weight * (shifted - jnp.log(safe_count))
    hinge_grad = (0.5 / block) * jnp.tanh(0.5 * shifted) + (0.5 / block)
    return jnp.where(count_block > 0, fitted, hinge_grad).astype(jnp.bfloat16)


def in_order(
    kernel, tokens, out_shape, in_specs, out_specs=None, grid=(), vmem=16, scalars=None, aliases={}
):
    ahead = scalars is not None

    def wrapped(*refs):
        done = refs[-1]
        done[...] = jnp.zeros_like(done)
        kernel(*refs[:ahead], *refs[ahead + len(tokens) : -1])

    done_spec = pl.BlockSpec((8, 128), lambda *ids: (0, 0)) if grid else whole
    out_specs = [whole] * len(out_shape) if out_specs is None else out_specs
    call = pl.pallas_call(
        wrapped,
        grid_spec=pltpu.PrefetchScalarGridSpec(
            num_scalar_prefetch=int(ahead),
            grid=grid,
            in_specs=[anywhere] * len(tokens) + list(in_specs),
            out_specs=list(out_specs) + [done_spec],
        ),
        out_shape=list(out_shape) + [done_shape],
        input_output_aliases=aliases,
        cost_estimate=small_cost,
        compiler_params=pltpu.CompilerParams(vmem_limit_bytes=vmem * MIB),
    )
    return lambda *args: call(*([scalars] if ahead else []), *held(tokens), *args)


def held(tokens):
    return [*map(lambda token: in_hbm(token)[0] if token.shape == (8, 128) else token, tokens)]


def in_vmem(*values):
    return [pltpu.with_memory_space_constraint(value, pltpu.VMEM) for value in values]


def in_hbm(*values):
    return [pltpu.with_memory_space_constraint(value, pltpu.HBM) for value in values]


def gated(values, tokens):
    return pl.pallas_call(
        lambda *refs: None,
        in_specs=[anywhere] * (len(values) + len(tokens)),
        out_specs=[anywhere] * len(values),
        out_shape=[jax.ShapeDtypeStruct(value.shape, value.dtype) for value in values],
        input_output_aliases={i: i for i in range(len(values))},
        cost_estimate=small_cost,
        compiler_params=pltpu.CompilerParams(vmem_limit_bytes=MIB),
    )(*values, *held(tokens))


def halve_kernel(whole_values, half_values):
    half_values[...] = whole_values[...].reshape(half_values.shape).astype(half_values.dtype)


def halved(values, start, rows, tokens):
    lead, width = values.shape[:-2], values.shape[-1]
    return in_order(
        halve_kernel,
        tokens,
        [jax.ShapeDtypeStruct((rows, width), jnp.bfloat16)],
        [
            pl.BlockSpec(
                (*lead, LANES, width),
                lambda step: (*[0] * len(lead), start // LANES + step, 0),
            )
        ],
        [pl.BlockSpec((LANES, width), lambda step: (step, 0))],
        grid=(rows // LANES,),
        vmem=4,
    )(*in_hbm(values))


def pick_kernel(slots, seat, own, near, far, cross, asked, kept):
    for first, out in ((5, asked), (3, kept)):
        for slot in range(slots):
            for away, ref in enumerate((own, near, far, cross)):

                @pl.when(seat[first + slot] == away)
                def _(ref=ref, out=out, slot=slot):
                    for unit in range(out.shape[0]):
                        out[unit, pl.ds(slot * LANES, LANES), :] = ref[pl.ds(unit * LANES, LANES), :]


def picked(seat, pieces, slots, tokens):
    size, width = pieces[0].shape
    shape = (size // LANES, slots * LANES, width)
    return in_order(
        functools.partial(pick_kernel, slots),
        tokens,
        [jax.ShapeDtypeStruct(shape, jnp.bfloat16)] * 2,
        [smalls] + [whole] * 4,
    )(seat, *in_hbm(pieces[0]), *pieces[1:])


def count_terms(count, row_term, col_logs, block):
    safe = jnp.maximum(count, 1).astype(jnp.float32)
    some = (0.1 / block) + (0.25 / block) * (safe * lax.rsqrt(safe))
    return jnp.where(count > 0, some, 0.0), jnp.log(safe) - (row_term + col_logs)


def block_terms(rows, cols, terms, block):
    predicted = [
        lax.dot_general(piece, cols, (((1,), (1,)), ((), ())), preferred_element_type=jnp.float32)
        for piece in rows
    ]
    cells = []
    for value, (weight, target) in zip(predicted, terms):
        error = value - target
        hinge_grad = (0.5 / block) * jnp.tanh(0.5 * error) + (0.5 / block)
        cells.append(jnp.where(weight > 0.0, weight * error, hinge_grad).astype(jnp.bfloat16))
    row_parts = [jnp.dot(cell, cols, preferred_element_type=jnp.float32) for cell in cells]
    col_parts = [
        lax.dot_general(cell, piece, (((0,), (0,)), ((), ())), preferred_element_type=jnp.float32)
        for cell, piece in zip(cells, rows)
    ]
    return row_parts, sum(col_parts[1:], col_parts[0])


def own_kernel(start, slots, seat, row_term, col_freq, own, core, chip, both, cols, *rest):
    counts, rest = rest[: 2 * slots], rest[2 * slots :]
    row_grads, (col_grad, weight, target) = rest[:4], rest[4:]
    step = pl.program_id(0)
    block, size = row_term.shape[0], own.shape[0]

    @pl.when(step == 0)
    def _():
        for row_grad in row_grads:
            row_grad[...] = jnp.zeros_like(row_grad)

    def logs(slot, which):
        at = seat[1 + slot] * block + (seat[0] ^ which) * (block // 2) + (start + step) * LANES
        return jnp.log(col_freq[:, pl.ds(pl.multiple_of(at, LANES), LANES)].astype(jnp.float32))

    col_logs = [[logs(slot, which) for slot in range(slots)] for which in range(2)]
    downs = [pl.ds(pl.multiple_of((seat[7] ^ p) * size, size), size) for p in range(4)]

    def side_terms(at, which):
        pairs = [
            count_terms(
                counts[which * slots + slot][0, 0, 0, at, :],
                row_term[at, :],
                col_logs[which][slot],
                block,
            )
            for slot in range(slots)
        ]
        return [jnp.concatenate(pair, axis=1) for pair in zip(*pairs)]

    row_parts, total = block_terms(
        [ref[...] for ref in (own, core, chip, both)],
        cols[0],
        [side_terms(at, 0) for at in downs],
        block,
    )
    for row_grad, row_part in zip(row_grads, row_parts):
        row_grad[...] += row_part
    col_grad[0] = total
    for at in downs:
        weight[step, at, :], target[step, at, :] = side_terms(at, 1)


def other_kernel(block, earlier, seat, own, core, chip, both, cols, weight, target, *rest):
    grads, sums = rest[: 4 + 4 * earlier], rest[4 + 4 * earlier : -1]
    col_grad = rest[-1]
    size = own.shape[0]
    downs = [pl.ds(pl.multiple_of((seat[7] ^ p) * size, size), size) for p in range(4)]
    for unit in range(cols.shape[0]):
        row_parts, total = block_terms(
            [ref[...] for ref in (own, core, chip, both)],
            cols[unit],
            [(weight[unit, at, :], target[unit, at, :]) for at in downs],
            block,
        )
        for piece, row_part in enumerate(row_parts):
            for before in [sums[piece]] if unit else grads[piece::4]:
                row_part = row_part + before[...]
            sums[piece][...] = row_part
        col_grad[unit] = total.astype(col_grad.dtype)


def own_grads(seat, row_term, col_freq, rows, cols, counts, start, tokens):
    size, width = rows[0].shape
    units, both, _ = cols.shape
    slots, block = counts.shape[2:4]
    halves = block // 2 // LANES
    grad_shape = pltpu.VMEM((size, width), jnp.float32)
    term_shape = pltpu.VMEM((units, block, both), jnp.float32)
    col_spec = pl.BlockSpec((1, both, width), lambda unit, seat: (unit, 0, 0))

    def count_spec(slot, which):
        return pl.BlockSpec(
            (1, 1, 1, block, LANES),
            lambda unit, seat: (0, 0, slot, 0, (seat[0] ^ which) * halves + start + unit),
        )

    count_specs = [count_spec(slot, which) for which in range(2) for slot in range(slots)]
    counts = pltpu.with_memory_space_constraint(counts, pltpu.HBM)
    return in_order(
        functools.partial(own_kernel, start, slots),
        tokens,
        [grad_shape] * 4 + [pltpu.HBM(cols.shape, jnp.float32), term_shape, term_shape],
        [whole] * 6 + [col_spec] + count_specs,
        [whole] * 4 + [col_spec, whole, whole],
        grid=(units,),
        vmem=32,
        scalars=seat,
    )(row_term, col_freq, *rows, cols, *[counts] * (2 * slots))


def other_grads(seat, rows, cols, weight, target, before, earlier, tokens):
    size, width = rows[0].shape
    grad_shape = jax.ShapeDtypeStruct((size, width), jnp.float32)
    return in_order(
        functools.partial(other_kernel, weight.shape[1], len(earlier)),
        tokens,
        [grad_shape] * 4 + [pltpu.HBM(cols.shape, jnp.bfloat16)],
        [smalls] + [whole] * (11 + 4 * len(earlier)),
        vmem=32,
    )(
        seat,
        *rows,
        cols,
        *in_vmem(weight, target, *before),
        *[grad for grads in earlier for grad in grads],
    )


def sum_kernel(slots, seat, mine, theirs, home, near, *rest):
    units = mine.shape[0]
    for unit in range(units):
        if len(rest) > 2:
            outs = home.at[unit], near.at[unit], rest[unit].at[0], rest[units + unit].at[0]
        else:
            outs = home.at[unit], near.at[unit], rest[0].at[unit], rest[1].at[unit]
        for away, out in enumerate(outs):
            total = jnp.zeros(out.shape, jnp.float32)
            for slot in range(slots):
                at = pl.ds(slot * LANES, LANES)
                total = total + jnp.where(seat[3 + slot] == away, mine[unit, at, :], 0.0)
                total = total + jnp.where(
                    seat[5 + slot] == away, theirs[unit, at, :].astype(jnp.float32), 0.0
                )
            out[...] = total.astype(out.dtype)


def block_sums(seat, mine, theirs, slots, split, tokens):
    units, _, width = mine.shape
    shape = (units, LANES, width)
    count, part = (units, (1, LANES, width)) if split else (1, shape)
    return in_order(
        functools.partial(sum_kernel, slots),
        tokens,
        [pltpu.HBM(shape, jnp.float32), pltpu.HBM(shape, jnp.bfloat16)]
        + [pltpu.HBM(part, jnp.float32)] * count
        + [jax.ShapeDtypeStruct(part, jnp.bfloat16)] * count,
        [smalls, whole, whole],
    )(seat, mine, theirs)


def relay_kernel(far, cross, out):
    out[...] = (far[...] + cross[...].astype(jnp.float32)).astype(out.dtype)


def relayed(far, cross, tokens):
    shape = jax.ShapeDtypeStruct(far.shape, jnp.bfloat16)
    return in_order(relay_kernel, tokens, [shape], [whole] * 2, vmem=4)(*in_hbm(far), cross)


def add_kernel(left, right, out):
    out[...] = (left[...] + right[...]).astype(out.dtype)


def added(left, right, tokens):
    shape = jax.ShapeDtypeStruct(left.shape, jnp.bfloat16)
    return in_order(add_kernel, tokens, [shape], [whole] * 2, vmem=4)(left, right)


def update_kernel(count, embed, accum, home, near, *rest):
    embed_new, accum_new = rest[-2:]
    far = rest[0][...]
    for unit in range(1, count):
        far = jnp.where(pl.program_id(0) == unit, rest[unit][...], far)
    grad = home[...] + near[...].astype(jnp.float32) + far.astype(jnp.float32)
    total = accum[...] + grad * grad
    accum_new[...] = total
    embed_new[...] = embed[...] - learn_rate * grad / jnp.sqrt(total)


def updated(embed, accum, start, sums, before, tokens):
    home, near, *fars = sums
    units, _, width = home.shape
    shape = jax.ShapeDtypeStruct(embed.shape, jnp.float32)
    outer = pl.BlockSpec((1, LANES, width), lambda unit: (0, start + unit, 0))
    inner = pl.BlockSpec((1, LANES, width), lambda unit: (unit, 0, 0))
    last = inner if len(fars) == 1 else pl.BlockSpec((1, LANES, width), lambda unit: (0, 0, 0))
    count = len(tokens) + 4 + len(fars)
    return in_order(
        functools.partial(update_kernel, len(fars)),
        tokens,
        [shape, shape],
        [outer, outer, inner, inner] + [last] * len(fars) + [anywhere] * len(before),
        [outer, outer],
        grid=(units,),
        vmem=8,
        aliases={count + i: i for i in range(len(before))},
    )(*in_hbm(embed, accum), *sums, *before)


def crossed_body(
    row_embed,
    row_accum,
    col_embed,
    col_accum,
    col_freq,
    row_freq,
    block_cols,
    counts,
    excluded,
    log_total,
):
    block = counts.shape[3]
    slots = counts.shape[2]
    width = col_embed.shape[2]
    row_index = lax.axis_index("row")
    col_index = lax.axis_index("col")
    half = row_index % 2
    home = row_index // 2

    mate_swap = [(i, i ^ 1) for i in range(8)]
    near_swap = [(i, i ^ 2) for i in range(8)]
    far_swap = [(i, i ^ 4) for i in range(8)]
    core_swap = [(i, i ^ 1) for i in range(4)]
    chip_swap = [(i, i ^ 2) for i in range(4)]

    def swap(name, value, axis, pairs):
        with jax.named_scope(name):
            return lax.ppermute(value, axis, pairs)

    chosen = block_cols[0, 0]
    mate_chosen = swap("mate_chosen", chosen, "row", mate_swap)
    seat = jnp.concatenate(
        [half[None], chosen, chosen ^ home, mate_chosen ^ home, col_index[None]]
    ).astype(jnp.int32)

    starts = [sum(CUTS[:part]) for part in range(len(CUTS))]

    def far_cols(part, own):
        far = swap(f"cols_far_{part}", own, "row", far_swap)
        return own, swap(f"cols_near_{part}", own, "row", near_swap), far

    def near_cols(part, own, near, far):
        return own, near, far, swap(f"cols_cross_{part}", far, "row", near_swap)

    cols = near_cols(0, *far_cols(0, col_embed[0, : CUTS[0] * LANES].astype(jnp.bfloat16)))
    row_half, done = halved(row_embed, 0, row_embed.shape[0], cols[:1])
    core_rows = swap("core_rows", row_half, "col", core_swap)
    chip_rows = swap("chip_rows", row_half, "col", chip_swap)
    both_rows = swap("both_rows", chip_rows, "col", core_swap)
    rows = (row_half, core_rows, chip_rows, both_rows)
    parts = len(CUTS)

    def own_cols(part, *tokens):
        if part >= parts:
            return None, tokens[0]
        return halved(col_embed, starts[part] * LANES, CUTS[part] * LANES, tokens)

    own_next, done = own_cols(1, done)
    coming = far_cols(1, *gated((own_next,), (*cols[1:3], done)))
    row_term = (jnp.log(row_freq.astype(jnp.float32)) - log_total)[:, None]

    def own(part, cols, done):
        *grads, col_grad, weight, target, done = own_grads(
            seat, row_term, col_freq, rows, cols, counts, starts[part], (done,)
        )
        return grads, col_grad, (weight, target), done

    def other(cols, terms, before, earlier, done):
        *grads, col_grad, done = other_grads(seat, rows, cols, *terms, before, earlier, (done,))
        return grads, col_grad, done

    row_grads, col_new, sent = [], (), None

    def pick_part(part, cols, coming, *tokens):
        if coming is not None:
            tokens += coming[2:]
        asked, kept, done = picked(seat, cols, slots, tokens)
        received = swap(f"cols_mate_{part}", asked, "row", mate_swap)
        after_next = None
        if coming is not None:
            cols = near_cols(part + 1, *coming[:2], *gated(coming[2:], (done,)))
            own_next, done = own_cols(part + 2, done)
            if own_next is not None:
                after_next = far_cols(part + 2, own_next)
        return kept, received, cols, after_next, done

    def sum_part(part, mine, from_mate, *tokens):
        split = part + 1 == parts
        home_sum, near, *rest, done = block_sums(seat, mine, from_mate, slots, split, tokens)
        count = len(rest) // 2
        cross = [
            swap(f"grads_cross_{part}_{i}", rest[count + i], "row", near_swap)
            for i in range(count)
        ]
        return (home_sum, near, rest[:count], cross), done

    def send_part(part, sums, *tokens):
        home_sum, near, (far,), (cross,) = sums
        far, done = relayed(far, cross, tokens)
        near = swap(f"grads_near_{part}", near, "row", near_swap)
        far = swap(f"grads_far_{part}", far, "row", far_swap)
        return (home_sum, near, far), done

    def update_part(start, sums, *tokens):
        *new, done = updated(col_embed, col_accum, start, sums, col_new, tokens)
        return new, done

    *_, cross = cols
    cols = (*cols[:3], *gated((cross,), (done,)))
    kept, received, cols, coming, done = pick_part(0, cols, coming, done, core_rows, both_rows)
    for part in range(parts):
        own_rows, mine, terms, done = own(part, kept, done)
        if part + 1 < parts:
            kept, received_next, cols, coming, done = pick_part(
                part + 1, cols, coming, done, received
            )
        earlier = row_grads if part + 1 == parts else []
        other_rows, theirs, done = other(received, terms, own_rows, earlier, done)
        from_mate = swap(f"grads_mate_{part}", theirs, "row", mate_swap)
        if part:
            if sent:
                col_new, done = update_part(starts[part - 2], sent, done)
            sums, done = sum_part(part - 1, *waiting, done)
            if part + 1 == parts:
                home_grad, core_grad, chip_grad, both_grad = other_rows
                both_core = swap("row_grads_both", both_grad, "col", core_swap)
                from_core = swap("row_grads_core", core_grad, "col", core_swap)
            extra = (both_core, from_core) if part + 1 == parts else ()
            sent, done = send_part(part - 1, sums, done, *extra)
        row_grads.append(other_rows)
        waiting = mine, from_mate
        received = received_next

    sums, done = sum_part(parts - 1, *waiting, done)
    chip_sum, row_done = added(chip_grad, both_core, (done,))
    from_chip = swap("row_grads_chip", chip_sum, "col", chip_swap)
    own_grad = home_grad + from_core + from_chip.astype(jnp.float32)
    row_new = row_updates(row_embed, row_accum, row_freq, excluded, block, own_grad)


    home_sum, near, fars, crosses = sums
    passed = gated(sent[:1], (*sent[1:], done)) if sent else ()
    far_sums = []
    for unit, (far, cross) in enumerate(zip(fars, crosses)):
        far, done = relayed(far, cross, (done, *passed))
        far_sums.append(swap(f"grads_far_{parts - 1}_{unit}", far, "row", far_swap))
    near = swap(f"grads_near_{parts - 1}", near, "row", near_swap)
    if sent:
        col_new, done = update_part(starts[parts - 2], (*passed, *sent[1:]), done)
    sums = home_sum, near, *far_sums
    col_new, done = update_part(starts[parts - 1], sums, done, row_new[1])
    return (*row_new, *col_new)


def row_updates(row_embed, row_accum, row_freq, excluded, block, own_grad):
    own_rows = row_embed.shape[0]
    col_index = lax.axis_index("col")
    row_index = lax.axis_index("row")
    own_freq = lax.dynamic_slice_in_dim(row_freq, col_index * own_rows, own_rows).astype(
        jnp.float32
    )
    row_ids = row_index * block + col_index * own_rows + jnp.arange(own_rows, dtype=jnp.int32)
    decayed = jnp.all(row_ids[:, None] != excluded[None, :], axis=1)
    freq_root = jnp.sqrt(own_freq)
    decay_coef = jnp.where(decayed, decay_rate * freq_root / (freq_root + 30.0), jnp.float32(0.0))
    full_grad = own_grad + decay_coef[:, None] * row_embed
    row_accum_new = row_accum + full_grad * full_grad
    row_embed_new = row_embed - learn_rate * full_grad / jnp.sqrt(row_accum_new)
    return row_embed_new, row_accum_new


def col_updates(col_embed, col_accum, col_grad):
    col_step = col_grad[None]
    col_accum_new = col_accum + col_step * col_step
    col_embed_new = col_embed - learn_rate * col_step / jnp.sqrt(col_accum_new)
    return col_embed_new, col_accum_new


def gathered_body(
    row_embed,
    row_accum,
    col_embed,
    col_accum,
    col_freq,
    row_freq,
    block_cols,
    counts,
    excluded,
    log_total,
):
    block = counts.shape[3]
    slots = counts.shape[2]
    width = row_embed.shape[1]
    chosen = block_cols[0, 0]
    block_rows = lax.all_gather(row_embed.astype(jnp.bfloat16), "col", axis=0, tiled=True)
    group = lax.all_gather(col_embed[0].astype(jnp.bfloat16), "row", axis=0, tiled=True)
    row_term = (jnp.log(row_freq.astype(jnp.float32)) - log_total)[:, None]
    col_logs = jnp.log(col_freq[0].astype(jnp.float32))
    row_grad = jnp.zeros((block, width), jnp.float32)
    summed = jnp.zeros(group.shape, jnp.float32)
    for slot in range(slots):
        start = chosen[slot] * block
        cols = lax.dynamic_slice_in_dim(group, start, block)
        predicted = lax.dot_general(
            block_rows, cols, (((1,), (1,)), ((), ())), preferred_element_type=jnp.float32
        )
        shifted = predicted + row_term + lax.dynamic_slice_in_dim(col_logs, start, block)[None]
        cell = cell_grads(counts[0, 0, slot], shifted, block)
        row_grad = row_grad + jnp.dot(cell, cols, preferred_element_type=jnp.float32)
        term = lax.dot_general(
            cell, block_rows, (((0,), (0,)), ((), ())), preferred_element_type=jnp.float32
        )
        summed = lax.dynamic_update_slice_in_dim(summed, term, start, 0)
    col_grad = lax.psum_scatter(summed, "row", scatter_dimension=0, tiled=True)
    own_grad = lax.psum_scatter(row_grad, "col", scatter_dimension=0, tiled=True)
    return (
        *row_updates(row_embed, row_accum, row_freq, excluded, block, own_grad),
        *col_updates(col_embed, col_accum, col_grad),
    )


def body(row_embed, row_accum, col_embed, col_accum, col_freq, row_freq, block_cols, counts, *rest):
    halves = lax.axis_size("row") == 8 and 2 * col_embed.shape[1] == counts.shape[3]
    pick = crossed_body if halves and lax.axis_size("col") == 4 else gathered_body
    return pick(
        row_embed, row_accum, col_embed, col_accum, col_freq, row_freq, block_cols, counts, *rest
    )


def solution(mesh):
    in_specs = (
        P(("row", "col"), None),
        P(("row", "col"), None),
        P("col", "row", None),
        P("col", "row", None),
        P("col", None),
        P("row"),
        P("row", "col", None),
        P("row", "col", None, None, None),
        P(),
        P(),
    )
    out_specs = (
        P(("row", "col"), None),
        P(("row", "col"), None),
        P("col", "row", None),
        P("col", "row", None),
    )
    return jax.shard_map(body, mesh=mesh, in_specs=in_specs, out_specs=out_specs, check_vma=False)
```

```python
import functools

import jax
import jax.numpy as jnp
from jax import lax
from jax.experimental import pallas as pl
from jax.experimental.pallas import tpu as pltpu
from jax.sharding import PartitionSpec as P

learn_rate = 0.2
decay_rate = 0.5

LANES = 128
CUTS = (2, 2)

small_cost = pl.CostEstimate(flops=1, bytes_accessed=1, transcendentals=0)
whole = pl.BlockSpec(memory_space=pltpu.VMEM)
smalls = pl.BlockSpec(memory_space=pltpu.SMEM)
anywhere = pl.BlockSpec(memory_space=pl.ANY)
done_shape = pltpu.HBM((8, 128), jnp.float32)
MIB = 1024 * 1024


def cell_grads(count_block, shifted, block):
    safe_count = jnp.maximum(count_block, 1).astype(jnp.float32)
    weight = (0.1 / block) + (0.25 / block) * jnp.sqrt(safe_count)
    fitted = weight * (shifted - jnp.log(safe_count))
    hinge_grad = (0.5 / block) * jnp.tanh(0.5 * shifted) + (0.5 / block)
    return jnp.where(count_block > 0, fitted, hinge_grad).astype(jnp.bfloat16)


def in_order(
    kernel, tokens, out_shape, in_specs, out_specs=None, grid=(), vmem=16, scalars=None, aliases={}
):
    ahead = scalars is not None

    def wrapped(*refs):
        done = refs[-1]
        done[...] = jnp.zeros_like(done)
        kernel(*refs[:ahead], *refs[ahead + len(tokens) : -1])

    done_spec = pl.BlockSpec((8, 128), lambda *ids: (0, 0)) if grid else whole
    out_specs = [whole] * len(out_shape) if out_specs is None else out_specs
    call = pl.pallas_call(
        wrapped,
        grid_spec=pltpu.PrefetchScalarGridSpec(
            num_scalar_prefetch=int(ahead),
            grid=grid,
            in_specs=[anywhere] * len(tokens) + list(in_specs),
            out_specs=list(out_specs) + [done_spec],
        ),
        out_shape=list(out_shape) + [done_shape],
        input_output_aliases=aliases,
        cost_estimate=small_cost,
        compiler_params=pltpu.CompilerParams(vmem_limit_bytes=vmem * MIB),
    )
    return lambda *args: call(*([scalars] if ahead else []), *held(tokens), *args)


def held(tokens):
    return [*map(lambda token: in_hbm(token)[0] if token.shape == (8, 128) else token, tokens)]


def in_vmem(*values):
    return [pltpu.with_memory_space_constraint(value, pltpu.VMEM) for value in values]


def in_hbm(*values):
    return [pltpu.with_memory_space_constraint(value, pltpu.HBM) for value in values]


def gated(values, tokens):
    return pl.pallas_call(
        lambda *refs: None,
        in_specs=[anywhere] * (len(values) + len(tokens)),
        out_specs=[anywhere] * len(values),
        out_shape=[jax.ShapeDtypeStruct(value.shape, value.dtype) for value in values],
        input_output_aliases={i: i for i in range(len(values))},
        cost_estimate=small_cost,
        compiler_params=pltpu.CompilerParams(vmem_limit_bytes=MIB),
    )(*values, *held(tokens))


def halve_kernel(whole_values, half_values):
    half_values[...] = whole_values[...].reshape(half_values.shape).astype(half_values.dtype)


def halved(values, start, rows, tokens):
    lead, width = values.shape[:-2], values.shape[-1]
    return in_order(
        halve_kernel,
        tokens,
        [jax.ShapeDtypeStruct((rows, width), jnp.bfloat16)],
        [
            pl.BlockSpec(
                (*lead, LANES, width),
                lambda step: (*[0] * len(lead), start // LANES + step, 0),
            )
        ],
        [pl.BlockSpec((LANES, width), lambda step: (step, 0))],
        grid=(rows // LANES,),
        vmem=4,
    )(*in_hbm(values))


def pick_kernel(slots, seat, own, near, far, cross, asked, kept):
    for first, out in ((5, asked), (3, kept)):
        for slot in range(slots):
            for away, ref in enumerate((own, near, far, cross)):

                @pl.when(seat[first + slot] == away)
                def _(ref=ref, out=out, slot=slot):
                    for unit in range(out.shape[0]):
                        out[unit, pl.ds(slot * LANES, LANES), :] = ref[pl.ds(unit * LANES, LANES), :]


def picked(seat, pieces, slots, tokens):
    size, width = pieces[0].shape
    shape = (size // LANES, slots * LANES, width)
    return in_order(
        functools.partial(pick_kernel, slots),
        tokens,
        [jax.ShapeDtypeStruct(shape, jnp.bfloat16)] * 2,
        [smalls] + [whole] * 4,
    )(seat, *in_hbm(pieces[0]), *pieces[1:])


def count_terms(count, row_term, col_logs, block):
    safe = jnp.maximum(count, 1).astype(jnp.float32)
    some = (0.1 / block) + (0.25 / block) * (safe * lax.rsqrt(safe))
    return jnp.where(count > 0, some, 0.0), jnp.log(safe) - (row_term + col_logs)


def block_terms(rows, cols, terms, block):
    predicted = [
        lax.dot_general(piece, cols, (((1,), (1,)), ((), ())), preferred_element_type=jnp.float32)
        for piece in rows
    ]
    cells = []
    for value, (weight, target) in zip(predicted, terms):
        error = value - target
        hinge_grad = (0.5 / block) * jnp.tanh(0.5 * error) + (0.5 / block)
        cells.append(jnp.where(weight > 0.0, weight * error, hinge_grad).astype(jnp.bfloat16))
    row_parts = [jnp.dot(cell, cols, preferred_element_type=jnp.float32) for cell in cells]
    col_parts = [
        lax.dot_general(cell, piece, (((0,), (0,)), ((), ())), preferred_element_type=jnp.float32)
        for cell, piece in zip(cells, rows)
    ]
    return row_parts, sum(col_parts[1:], col_parts[0])


def own_kernel(start, slots, seat, row_term, col_freq, own, core, chip, both, cols, *rest):
    counts, rest = rest[: 2 * slots], rest[2 * slots :]
    row_grads, (col_grad, weight, target) = rest[:4], rest[4:]
    step = pl.program_id(0)
    block, size = row_term.shape[0], own.shape[0]

    @pl.when(step == 0)
    def _():
        for row_grad in row_grads:
            row_grad[...] = jnp.zeros_like(row_grad)

    def logs(slot, which):
        at = seat[1 + slot] * block + (seat[0] ^ which) * (block // 2) + (start + step) * LANES
        return jnp.log(col_freq[:, pl.ds(pl.multiple_of(at, LANES), LANES)].astype(jnp.float32))

    col_logs = [[logs(slot, which) for slot in range(slots)] for which in range(2)]
    downs = [pl.ds(pl.multiple_of((seat[7] ^ p) * size, size), size) for p in range(4)]

    def side_terms(at, which):
        pairs = [
            count_terms(
                counts[which * slots + slot][0, 0, 0, at, :],
                row_term[at, :],
                col_logs[which][slot],
                block,
            )
            for slot in range(slots)
        ]
        return [jnp.concatenate(pair, axis=1) for pair in zip(*pairs)]

    row_parts, total = block_terms(
        [ref[...] for ref in (own, core, chip, both)],
        cols[0],
        [side_terms(at, 0) for at in downs],
        block,
    )
    for row_grad, row_part in zip(row_grads, row_parts):
        row_grad[...] += row_part
    col_grad[0] = total
    for at in downs:
        weight[step, at, :], target[step, at, :] = side_terms(at, 1)


def other_kernel(block, earlier, seat, own, core, chip, both, cols, weight, target, *rest):
    grads, sums = rest[: 4 + 4 * earlier], rest[4 + 4 * earlier : -1]
    col_grad = rest[-1]
    size = own.shape[0]
    downs = [pl.ds(pl.multiple_of((seat[7] ^ p) * size, size), size) for p in range(4)]
    for unit in range(cols.shape[0]):
        row_parts, total = block_terms(
            [ref[...] for ref in (own, core, chip, both)],
            cols[unit],
            [(weight[unit, at, :], target[unit, at, :]) for at in downs],
            block,
        )
        for piece, row_part in enumerate(row_parts):
            for before in [sums[piece]] if unit else grads[piece::4]:
                row_part = row_part + before[...]
            sums[piece][...] = row_part
        col_grad[unit] = total.astype(col_grad.dtype)


def own_grads(seat, row_term, col_freq, rows, cols, counts, start, tokens):
    size, width = rows[0].shape
    units, both, _ = cols.shape
    slots, block = counts.shape[2:4]
    halves = block // 2 // LANES
    grad_shape = pltpu.VMEM((size, width), jnp.float32)
    term_shape = pltpu.VMEM((units, block, both), jnp.float32)
    col_spec = pl.BlockSpec((1, both, width), lambda unit, seat: (unit, 0, 0))

    def count_spec(slot, which):
        return pl.BlockSpec(
            (1, 1, 1, block, LANES),
            lambda unit, seat: (0, 0, slot, 0, (seat[0] ^ which) * halves + start + unit),
        )

    count_specs = [count_spec(slot, which) for which in range(2) for slot in range(slots)]
    counts = pltpu.with_memory_space_constraint(counts, pltpu.HBM)
    return in_order(
        functools.partial(own_kernel, start, slots),
        tokens,
        [grad_shape] * 4 + [pltpu.HBM(cols.shape, jnp.float32), term_shape, term_shape],
        [whole] * 6 + [col_spec] + count_specs,
        [whole] * 4 + [col_spec, whole, whole],
        grid=(units,),
        vmem=32,
        scalars=seat,
    )(row_term, col_freq, *rows, cols, *[counts] * (2 * slots))


def other_grads(seat, rows, cols, weight, target, before, earlier, tokens):
    size, width = rows[0].shape
    grad_shape = jax.ShapeDtypeStruct((size, width), jnp.float32)
    return in_order(
        functools.partial(other_kernel, weight.shape[1], len(earlier)),
        tokens,
        [grad_shape] * 4 + [pltpu.HBM(cols.shape, jnp.bfloat16)],
        [smalls] + [whole] * (11 + 4 * len(earlier)),
        vmem=32,
    )(
        seat,
        *rows,
        cols,
        *in_vmem(weight, target, *before),
        *[grad for grads in earlier for grad in grads],
    )


def sum_kernel(slots, seat, mine, theirs, home, near, *rest):
    units = mine.shape[0]
    for unit in range(units):
        if len(rest) > 2:
            outs = home.at[unit], near.at[unit], rest[unit].at[0], rest[units + unit].at[0]
        else:
            outs = home.at[unit], near.at[unit], rest[0].at[unit], rest[1].at[unit]
        for away, out in enumerate(outs):
            total = jnp.zeros(out.shape, jnp.float32)
            for slot in range(slots):
                at = pl.ds(slot * LANES, LANES)
                total = total + jnp.where(seat[3 + slot] == away, mine[unit, at, :], 0.0)
                total = total + jnp.where(
                    seat[5 + slot] == away, theirs[unit, at, :].astype(jnp.float32), 0.0
                )
            out[...] = total.astype(out.dtype)


def block_sums(seat, mine, theirs, slots, split, tokens):
    units, _, width = mine.shape
    shape = (units, LANES, width)
    count, part = (units, (1, LANES, width)) if split else (1, shape)
    return in_order(
        functools.partial(sum_kernel, slots),
        tokens,
        [pltpu.HBM(shape, jnp.float32), pltpu.HBM(shape, jnp.bfloat16)]
        + [pltpu.HBM(part, jnp.float32)] * count
        + [jax.ShapeDtypeStruct(part, jnp.bfloat16)] * count,
        [smalls, whole, whole],
    )(seat, mine, theirs)


def relay_kernel(far, cross, out):
    out[...] = (far[...] + cross[...].astype(jnp.float32)).astype(out.dtype)


def relayed(far, cross, tokens):
    shape = jax.ShapeDtypeStruct(far.shape, jnp.bfloat16)
    return in_order(relay_kernel, tokens, [shape], [whole] * 2, vmem=4)(*in_hbm(far), cross)


def add_kernel(left, right, out):
    out[...] = (left[...] + right[...]).astype(out.dtype)


def added(left, right, tokens):
    shape = jax.ShapeDtypeStruct(left.shape, jnp.bfloat16)
    return in_order(add_kernel, tokens, [shape], [whole] * 2, vmem=4)(left, right)


def update_kernel(count, embed, accum, home, near, *rest):
    embed_new, accum_new = rest[-2:]
    far = rest[0][...]
    for unit in range(1, count):
        far = jnp.where(pl.program_id(0) == unit, rest[unit][...], far)
    grad = home[...] + near[...].astype(jnp.float32) + far.astype(jnp.float32)
    total = accum[...] + grad * grad
    accum_new[...] = total
    embed_new[...] = embed[...] - learn_rate * grad / jnp.sqrt(total)


def updated(embed, accum, start, sums, before, tokens):
    home, near, *fars = sums
    units, _, width = home.shape
    shape = jax.ShapeDtypeStruct(embed.shape, jnp.float32)
    outer = pl.BlockSpec((1, LANES, width), lambda unit: (0, start + unit, 0))
    inner = pl.BlockSpec((1, LANES, width), lambda unit: (unit, 0, 0))
    last = inner if len(fars) == 1 else pl.BlockSpec((1, LANES, width), lambda unit: (0, 0, 0))
    count = len(tokens) + 4 + len(fars)
    return in_order(
        functools.partial(update_kernel, len(fars)),
        tokens,
        [shape, shape],
        [outer, outer, inner, inner] + [last] * len(fars) + [anywhere] * len(before),
        [outer, outer],
        grid=(units,),
        vmem=8,
        aliases={count + i: i for i in range(len(before))},
    )(*in_hbm(embed, accum), *sums, *before)


def crossed_body(
    row_embed,
    row_accum,
    col_embed,
    col_accum,
    col_freq,
    row_freq,
    block_cols,
    counts,
    excluded,
    log_total,
):
    block = counts.shape[3]
    slots = counts.shape[2]
    width = col_embed.shape[2]
    row_index = lax.axis_index("row")
    col_index = lax.axis_index("col")
    half = row_index % 2
    home = row_index // 2

    mate_swap = [(i, i ^ 1) for i in range(8)]
    near_swap = [(i, i ^ 2) for i in range(8)]
    far_swap = [(i, i ^ 4) for i in range(8)]
    core_swap = [(i, i ^ 1) for i in range(4)]
    chip_swap = [(i, i ^ 2) for i in range(4)]

    def swap(name, value, axis, pairs):
        with jax.named_scope(name):
            return lax.ppermute(value, axis, pairs)

    chosen = block_cols[0, 0]
    mate_chosen = swap("mate_chosen", chosen, "row", mate_swap)
    seat = jnp.concatenate(
        [half[None], chosen, chosen ^ home, mate_chosen ^ home, col_index[None]]
    ).astype(jnp.int32)

    starts = [sum(CUTS[:part]) for part in range(len(CUTS))]

    def far_cols(part, own):
        far = swap(f"cols_far_{part}", own, "row", far_swap)
        return own, swap(f"cols_near_{part}", own, "row", near_swap), far

    def near_cols(part, own, near, far):
        return own, near, far, swap(f"cols_cross_{part}", far, "row", near_swap)

    cols = near_cols(0, *far_cols(0, col_embed[0, : CUTS[0] * LANES].astype(jnp.bfloat16)))
    row_half, done = halved(row_embed, 0, row_embed.shape[0], cols[:1])
    core_rows = swap("core_rows", row_half, "col", core_swap)
    chip_rows = swap("chip_rows", row_half, "col", chip_swap)
    both_rows = swap("both_rows", chip_rows, "col", core_swap)
    rows = (row_half, core_rows, chip_rows, both_rows)
    parts = len(CUTS)

    def own_cols(part, *tokens):
        if part >= parts:
            return None, tokens[0]
        return halved(col_embed, starts[part] * LANES, CUTS[part] * LANES, tokens)

    own_next, done = own_cols(1, done)
    coming = far_cols(1, *gated((own_next,), (*cols[1:3], done)))
    row_term = (jnp.log(row_freq.astype(jnp.float32)) - log_total)[:, None]

    def own(part, cols, done):
        *grads, col_grad, weight, target, done = own_grads(
            seat, row_term, col_freq, rows, cols, counts, starts[part], (done,)
        )
        return grads, col_grad, (weight, target), done

    def other(cols, terms, before, earlier, done):
        *grads, col_grad, done = other_grads(seat, rows, cols, *terms, before, earlier, (done,))
        return grads, col_grad, done

    row_grads, col_new, sent = [], (), None

    def pick_part(part, cols, coming, *tokens):
        if coming is not None:
            tokens += coming[2:]
        asked, kept, done = picked(seat, cols, slots, tokens)
        received = swap(f"cols_mate_{part}", asked, "row", mate_swap)
        after_next = None
        if coming is not None:
            cols = near_cols(part + 1, *coming[:2], *gated(coming[2:], (done,)))
            own_next, done = own_cols(part + 2, done)
            if own_next is not None:
                after_next = far_cols(part + 2, own_next)
        return kept, received, cols, after_next, done

    def sum_part(part, mine, from_mate, *tokens):
        split = part + 1 == parts
        home_sum, near, *rest, done = block_sums(seat, mine, from_mate, slots, split, tokens)
        count = len(rest) // 2
        cross = [
            swap(f"grads_cross_{part}_{i}", rest[count + i], "row", near_swap)
            for i in range(count)
        ]
        return (home_sum, near, rest[:count], cross), done

    def send_part(part, sums, *tokens):
        home_sum, near, (far,), (cross,) = sums
        far, done = relayed(far, cross, tokens)
        near = swap(f"grads_near_{part}", near, "row", near_swap)
        far = swap(f"grads_far_{part}", far, "row", far_swap)
        return (home_sum, near, far), done

    def update_part(start, sums, *tokens):
        *new, done = updated(col_embed, col_accum, start, sums, col_new, tokens)
        return new, done

    *_, cross = cols
    cols = (*cols[:3], *gated((cross,), (done,)))
    kept, received, cols, coming, done = pick_part(0, cols, coming, done, core_rows, both_rows)
    for part in range(parts):
        own_rows, mine, terms, done = own(part, kept, done)
        if part + 1 < parts:
            kept, received_next, cols, coming, done = pick_part(
                part + 1, cols, coming, done
            )
        earlier = row_grads if part + 1 == parts else []
        other_rows, theirs, done = other(received, terms, own_rows, earlier, done)
        from_mate = swap(f"grads_mate_{part}", theirs, "row", mate_swap)
        if part:
            if sent:
                col_new, done = update_part(starts[part - 2], sent, done)
            sums, done = sum_part(part - 1, *waiting, done)
            if part + 1 == parts:
                home_grad, core_grad, chip_grad, both_grad = other_rows
                both_core = swap("row_grads_both", both_grad, "col", core_swap)
                from_core = swap("row_grads_core", core_grad, "col", core_swap)
            extra = (both_core, from_core) if part + 1 == parts else ()
            sent, done = send_part(part - 1, sums, done, *extra)
        row_grads.append(other_rows)
        waiting = mine, from_mate
        received = received_next

    sums, done = sum_part(parts - 1, *waiting, done)
    chip_sum, row_done = added(chip_grad, both_core, (done,))
    from_chip = swap("row_grads_chip", chip_sum, "col", chip_swap)
    own_grad = home_grad + from_core + from_chip.astype(jnp.float32)
    row_new = row_updates(row_embed, row_accum, row_freq, excluded, block, own_grad)


    home_sum, near, fars, crosses = sums
    passed = gated(sent[:1], (*sent[1:], done)) if sent else ()
    far_sums = []
    for unit, (far, cross) in enumerate(zip(fars, crosses)):
        far, done = relayed(far, cross, (done, *passed))
        far_sums.append(swap(f"grads_far_{parts - 1}_{unit}", far, "row", far_swap))
    near = swap(f"grads_near_{parts - 1}", near, "row", near_swap)
    if sent:
        col_new, done = update_part(starts[parts - 2], (*passed, *sent[1:]), done)
    sums = home_sum, near, *far_sums
    col_new, done = update_part(starts[parts - 1], sums, done, row_new[1])
    return (*row_new, *col_new)


def row_updates(row_embed, row_accum, row_freq, excluded, block, own_grad):
    own_rows = row_embed.shape[0]
    col_index = lax.axis_index("col")
    row_index = lax.axis_index("row")
    own_freq = lax.dynamic_slice_in_dim(row_freq, col_index * own_rows, own_rows).astype(
        jnp.float32
    )
    row_ids = row_index * block + col_index * own_rows + jnp.arange(own_rows, dtype=jnp.int32)
    decayed = jnp.all(row_ids[:, None] != excluded[None, :], axis=1)
    freq_root = jnp.sqrt(own_freq)
    decay_coef = jnp.where(decayed, decay_rate * freq_root / (freq_root + 30.0), jnp.float32(0.0))
    full_grad = own_grad + decay_coef[:, None] * row_embed
    row_accum_new = row_accum + full_grad * full_grad
    row_embed_new = row_embed - learn_rate * full_grad / jnp.sqrt(row_accum_new)
    return row_embed_new, row_accum_new


def col_updates(col_embed, col_accum, col_grad):
    col_step = col_grad[None]
    col_accum_new = col_accum + col_step * col_step
    col_embed_new = col_embed - learn_rate * col_step / jnp.sqrt(col_accum_new)
    return col_embed_new, col_accum_new


def gathered_body(
    row_embed,
    row_accum,
    col_embed,
    col_accum,
    col_freq,
    row_freq,
    block_cols,
    counts,
    excluded,
    log_total,
):
    block = counts.shape[3]
    slots = counts.shape[2]
    width = row_embed.shape[1]
    chosen = block_cols[0, 0]
    block_rows = lax.all_gather(row_embed.astype(jnp.bfloat16), "col", axis=0, tiled=True)
    group = lax.all_gather(col_embed[0].astype(jnp.bfloat16), "row", axis=0, tiled=True)
    row_term = (jnp.log(row_freq.astype(jnp.float32)) - log_total)[:, None]
    col_logs = jnp.log(col_freq[0].astype(jnp.float32))
    row_grad = jnp.zeros((block, width), jnp.float32)
    summed = jnp.zeros(group.shape, jnp.float32)
    for slot in range(slots):
        start = chosen[slot] * block
        cols = lax.dynamic_slice_in_dim(group, start, block)
        predicted = lax.dot_general(
            block_rows, cols, (((1,), (1,)), ((), ())), preferred_element_type=jnp.float32
        )
        shifted = predicted + row_term + lax.dynamic_slice_in_dim(col_logs, start, block)[None]
        cell = cell_grads(counts[0, 0, slot], shifted, block)
        row_grad = row_grad + jnp.dot(cell, cols, preferred_element_type=jnp.float32)
        term = lax.dot_general(
            cell, block_rows, (((0,), (0,)), ((), ())), preferred_element_type=jnp.float32
        )
        summed = lax.dynamic_update_slice_in_dim(summed, term, start, 0)
    col_grad = lax.psum_scatter(summed, "row", scatter_dimension=0, tiled=True)
    own_grad = lax.psum_scatter(row_grad, "col", scatter_dimension=0, tiled=True)
    return (
        *row_updates(row_embed, row_accum, row_freq, excluded, block, own_grad),
        *col_updates(col_embed, col_accum, col_grad),
    )


def body(row_embed, row_accum, col_embed, col_accum, col_freq, row_freq, block_cols, counts, *rest):
    halves = lax.axis_size("row") == 8 and 2 * col_embed.shape[1] == counts.shape[3]
    pick = crossed_body if halves and lax.axis_size("col") == 4 else gathered_body
    return pick(
        row_embed, row_accum, col_embed, col_accum, col_freq, row_freq, block_cols, counts, *rest
    )


def solution(mesh):
    in_specs = (
        P(("row", "col"), None),
        P(("row", "col"), None),
        P("col", "row", None),
        P("col", "row", None),
        P("col", None),
        P("row"),
        P("row", "col", None),
        P("row", "col", None, None, None),
        P(),
        P(),
    )
    out_specs = (
        P(("row", "col"), None),
        P(("row", "col"), None),
        P("col", "row", None),
        P("col", "row", None),
    )
    return jax.shard_map(body, mesh=mesh, in_specs=in_specs, out_specs=out_specs, check_vma=False)
```

```python
import functools

import jax
import jax.numpy as jnp
from jax import lax
from jax.experimental import pallas as pl
from jax.experimental.pallas import tpu as pltpu
from jax.sharding import PartitionSpec as P

learn_rate = 0.2
decay_rate = 0.5

LANES = 128
CUTS = (2, 2)

small_cost = pl.CostEstimate(flops=1, bytes_accessed=1, transcendentals=0)
whole = pl.BlockSpec(memory_space=pltpu.VMEM)
smalls = pl.BlockSpec(memory_space=pltpu.SMEM)
anywhere = pl.BlockSpec(memory_space=pl.ANY)
done_shape = pltpu.HBM((8, 128), jnp.float32)
MIB = 1024 * 1024


def cell_grads(count_block, shifted, block):
    safe_count = jnp.maximum(count_block, 1).astype(jnp.float32)
    weight = (0.1 / block) + (0.25 / block) * jnp.sqrt(safe_count)
    fitted = weight * (shifted - jnp.log(safe_count))
    hinge_grad = (0.5 / block) * jnp.tanh(0.5 * shifted) + (0.5 / block)
    return jnp.where(count_block > 0, fitted, hinge_grad).astype(jnp.bfloat16)


def in_order(
    kernel, tokens, out_shape, in_specs, out_specs=None, grid=(), vmem=16, scalars=None, aliases={}
):
    ahead = scalars is not None

    def wrapped(*refs):
        done = refs[-1]
        done[...] = jnp.zeros_like(done)
        kernel(*refs[:ahead], *refs[ahead + len(tokens) : -1])

    done_spec = pl.BlockSpec((8, 128), lambda *ids: (0, 0)) if grid else whole
    out_specs = [whole] * len(out_shape) if out_specs is None else out_specs
    call = pl.pallas_call(
        wrapped,
        grid_spec=pltpu.PrefetchScalarGridSpec(
            num_scalar_prefetch=int(ahead),
            grid=grid,
            in_specs=[anywhere] * len(tokens) + list(in_specs),
            out_specs=list(out_specs) + [done_spec],
        ),
        out_shape=list(out_shape) + [done_shape],
        input_output_aliases=aliases,
        cost_estimate=small_cost,
        compiler_params=pltpu.CompilerParams(vmem_limit_bytes=vmem * MIB),
    )
    return lambda *args: call(*([scalars] if ahead else []), *held(tokens), *args)


def held(tokens):
    return [*map(lambda token: in_hbm(token)[0] if token.shape == (8, 128) else token, tokens)]


def in_vmem(*values):
    return [pltpu.with_memory_space_constraint(value, pltpu.VMEM) for value in values]


def in_hbm(*values):
    return [pltpu.with_memory_space_constraint(value, pltpu.HBM) for value in values]


def gated(values, tokens):
    return pl.pallas_call(
        lambda *refs: None,
        in_specs=[anywhere] * (len(values) + len(tokens)),
        out_specs=[anywhere] * len(values),
        out_shape=[jax.ShapeDtypeStruct(value.shape, value.dtype) for value in values],
        input_output_aliases={i: i for i in range(len(values))},
        cost_estimate=small_cost,
        compiler_params=pltpu.CompilerParams(vmem_limit_bytes=MIB),
    )(*values, *held(tokens))


def halve_kernel(whole_values, half_values):
    half_values[...] = whole_values[...].reshape(half_values.shape).astype(half_values.dtype)


def halved(values, start, rows, tokens):
    lead, width = values.shape[:-2], values.shape[-1]
    return in_order(
        halve_kernel,
        tokens,
        [jax.ShapeDtypeStruct((rows, width), jnp.bfloat16)],
        [
            pl.BlockSpec(
                (*lead, LANES, width),
                lambda step: (*[0] * len(lead), start // LANES + step, 0),
            )
        ],
        [pl.BlockSpec((LANES, width), lambda step: (step, 0))],
        grid=(rows // LANES,),
        vmem=4,
    )(*in_hbm(values))


def pick_kernel(slots, seat, own, near, far, cross, asked, kept):
    for first, out in ((5, asked), (3, kept)):
        for slot in range(slots):
            for away, ref in enumerate((own, near, far, cross)):

                @pl.when(seat[first + slot] == away)
                def _(ref=ref, out=out, slot=slot):
                    for unit in range(out.shape[0]):
                        out[unit, pl.ds(slot * LANES, LANES), :] = ref[pl.ds(unit * LANES, LANES), :]


def picked(seat, pieces, slots, tokens):
    size, width = pieces[0].shape
    shape = (size // LANES, slots * LANES, width)
    return in_order(
        functools.partial(pick_kernel, slots),
        tokens,
        [jax.ShapeDtypeStruct(shape, jnp.bfloat16)] * 2,
        [smalls] + [whole] * 4,
    )(seat, *in_hbm(pieces[0]), *pieces[1:])


def count_terms(count, row_term, col_logs, block):
    safe = jnp.maximum(count, 1).astype(jnp.float32)
    some = (0.1 / block) + (0.25 / block) * (safe * lax.rsqrt(safe))
    return jnp.where(count > 0, some, 0.0), jnp.log(safe) - (row_term + col_logs)


def block_terms(rows, cols, terms, block):
    predicted = [
        lax.dot_general(piece, cols, (((1,), (1,)), ((), ())), preferred_element_type=jnp.float32)
        for piece in rows
    ]
    cells = []
    for value, (weight, target) in zip(predicted, terms):
        error = value - target
        hinge_grad = (0.5 / block) * jnp.tanh(0.5 * error) + (0.5 / block)
        cells.append(jnp.where(weight > 0.0, weight * error, hinge_grad).astype(jnp.bfloat16))
    row_parts = [jnp.dot(cell, cols, preferred_element_type=jnp.float32) for cell in cells]
    col_parts = [
        lax.dot_general(cell, piece, (((0,), (0,)), ((), ())), preferred_element_type=jnp.float32)
        for cell, piece in zip(cells, rows)
    ]
    return row_parts, sum(col_parts[1:], col_parts[0])


def own_kernel(start, slots, seat, row_term, col_freq, own, core, chip, both, cols, *rest):
    counts, rest = rest[: 2 * slots], rest[2 * slots :]
    row_grads, (col_grad, weight, target) = rest[:4], rest[4:]
    step = pl.program_id(0)
    block, size = row_term.shape[0], own.shape[0]

    @pl.when(step == 0)
    def _():
        for row_grad in row_grads:
            row_grad[...] = jnp.zeros_like(row_grad)

    def logs(slot, which):
        at = seat[1 + slot] * block + (seat[0] ^ which) * (block // 2) + (start + step) * LANES
        return jnp.log(col_freq[:, pl.ds(pl.multiple_of(at, LANES), LANES)].astype(jnp.float32))

    col_logs = [[logs(slot, which) for slot in range(slots)] for which in range(2)]
    downs = [pl.ds(pl.multiple_of((seat[7] ^ p) * size, size), size) for p in range(4)]

    def side_terms(at, which):
        pairs = [
            count_terms(
                counts[which * slots + slot][0, 0, 0, at, :],
                row_term[at, :],
                col_logs[which][slot],
                block,
            )
            for slot in range(slots)
        ]
        return [jnp.concatenate(pair, axis=1) for pair in zip(*pairs)]

    row_parts, total = block_terms(
        [ref[...] for ref in (own, core, chip, both)],
        cols[0],
        [side_terms(at, 0) for at in downs],
        block,
    )
    for row_grad, row_part in zip(row_grads, row_parts):
        row_grad[...] += row_part
    col_grad[0] = total
    for at in downs:
        weight[step, at, :], target[step, at, :] = side_terms(at, 1)


def other_kernel(block, earlier, seat, own, core, chip, both, cols, weight, target, *rest):
    grads, sums = rest[: 4 + 4 * earlier], rest[4 + 4 * earlier : -1]
    col_grad = rest[-1]
    size = own.shape[0]
    downs = [pl.ds(pl.multiple_of((seat[7] ^ p) * size, size), size) for p in range(4)]
    for unit in range(cols.shape[0]):
        row_parts, total = block_terms(
            [ref[...] for ref in (own, core, chip, both)],
            cols[unit],
            [(weight[unit, at, :], target[unit, at, :]) for at in downs],
            block,
        )
        for piece, row_part in enumerate(row_parts):
            for before in [sums[piece]] if unit else grads[piece::4]:
                row_part = row_part + before[...]
            sums[piece][...] = row_part
        col_grad[unit] = total.astype(col_grad.dtype)


def own_grads(seat, row_term, col_freq, rows, cols, counts, start, tokens):
    size, width = rows[0].shape
    units, both, _ = cols.shape
    slots, block = counts.shape[2:4]
    halves = block // 2 // LANES
    grad_shape = pltpu.VMEM((size, width), jnp.float32)
    term_shape = pltpu.VMEM((units, block, both), jnp.float32)
    col_spec = pl.BlockSpec((1, both, width), lambda unit, seat: (unit, 0, 0))

    def count_spec(slot, which):
        return pl.BlockSpec(
            (1, 1, 1, block, LANES),
            lambda unit, seat: (0, 0, slot, 0, (seat[0] ^ which) * halves + start + unit),
        )

    count_specs = [count_spec(slot, which) for which in range(2) for slot in range(slots)]
    counts = pltpu.with_memory_space_constraint(counts, pltpu.HBM)
    return in_order(
        functools.partial(own_kernel, start, slots),
        tokens,
        [grad_shape] * 4 + [pltpu.HBM(cols.shape, jnp.float32), term_shape, term_shape],
        [whole] * 6 + [col_spec] + count_specs,
        [whole] * 4 + [col_spec, whole, whole],
        grid=(units,),
        vmem=32,
        scalars=seat,
    )(row_term, col_freq, *rows, cols, *[counts] * (2 * slots))


def other_grads(seat, rows, cols, weight, target, before, earlier, tokens):
    size, width = rows[0].shape
    grad_shape = jax.ShapeDtypeStruct((size, width), jnp.float32)
    return in_order(
        functools.partial(other_kernel, weight.shape[1], len(earlier)),
        tokens,
        [grad_shape] * 4 + [pltpu.HBM(cols.shape, jnp.bfloat16)],
        [smalls] + [whole] * (11 + 4 * len(earlier)),
        vmem=32,
    )(
        seat,
        *rows,
        cols,
        *in_vmem(weight, target, *before),
        *[grad for grads in earlier for grad in grads],
    )


def sum_kernel(slots, seat, mine, theirs, home, near, *rest):
    units = mine.shape[0]
    for unit in range(units):
        if len(rest) > 2:
            outs = home.at[unit], near.at[unit], rest[unit].at[0], rest[units + unit].at[0]
        else:
            outs = home.at[unit], near.at[unit], rest[0].at[unit], rest[1].at[unit]
        for away, out in enumerate(outs):
            total = jnp.zeros(out.shape, jnp.float32)
            for slot in range(slots):
                at = pl.ds(slot * LANES, LANES)
                total = total + jnp.where(seat[3 + slot] == away, mine[unit, at, :], 0.0)
                total = total + jnp.where(
                    seat[5 + slot] == away, theirs[unit, at, :].astype(jnp.float32), 0.0
                )
            out[...] = total.astype(out.dtype)


def block_sums(seat, mine, theirs, slots, split, tokens):
    units, _, width = mine.shape
    shape = (units, LANES, width)
    count, part = (units, (1, LANES, width)) if split else (1, shape)
    return in_order(
        functools.partial(sum_kernel, slots),
        tokens,
        [pltpu.HBM(shape, jnp.float32), pltpu.HBM(shape, jnp.bfloat16)]
        + [pltpu.HBM(part, jnp.float32)] * count
        + [jax.ShapeDtypeStruct(part, jnp.bfloat16)] * count,
        [smalls, whole, whole],
    )(seat, mine, theirs)


def relay_kernel(far, cross, out):
    out[...] = (far[...] + cross[...].astype(jnp.float32)).astype(out.dtype)


def relayed(far, cross, tokens):
    shape = jax.ShapeDtypeStruct(far.shape, jnp.bfloat16)
    return in_order(relay_kernel, tokens, [shape], [whole] * 2, vmem=4)(*in_hbm(far), cross)


def add_kernel(left, right, out):
    out[...] = (left[...] + right[...]).astype(out.dtype)


def added(left, right, tokens):
    shape = jax.ShapeDtypeStruct(left.shape, jnp.bfloat16)
    return in_order(add_kernel, tokens, [shape], [whole] * 2, vmem=4)(left, right)


def update_kernel(count, embed, accum, home, near, *rest):
    embed_new, accum_new = rest[-2:]
    far = rest[0][...]
    for unit in range(1, count):
        far = jnp.where(pl.program_id(0) == unit, rest[unit][...], far)
    grad = home[...] + near[...].astype(jnp.float32) + far.astype(jnp.float32)
    total = accum[...] + grad * grad
    accum_new[...] = total
    embed_new[...] = embed[...] - learn_rate * grad / jnp.sqrt(total)


def updated(embed, accum, start, sums, before, tokens):
    home, near, *fars = sums
    units, _, width = home.shape
    shape = jax.ShapeDtypeStruct(embed.shape, jnp.float32)
    outer = pl.BlockSpec((1, LANES, width), lambda unit: (0, start + unit, 0))
    inner = pl.BlockSpec((1, LANES, width), lambda unit: (unit, 0, 0))
    last = inner if len(fars) == 1 else pl.BlockSpec((1, LANES, width), lambda unit: (0, 0, 0))
    count = len(tokens) + 4 + len(fars)
    return in_order(
        functools.partial(update_kernel, len(fars)),
        tokens,
        [shape, shape],
        [outer, outer, inner, inner] + [last] * len(fars) + [anywhere] * len(before),
        [outer, outer],
        grid=(units,),
        vmem=8,
        aliases={count + i: i for i in range(len(before))},
    )(*in_hbm(embed, accum), *sums, *before)


def crossed_body(
    row_embed,
    row_accum,
    col_embed,
    col_accum,
    col_freq,
    row_freq,
    block_cols,
    counts,
    excluded,
    log_total,
):
    block = counts.shape[3]
    slots = counts.shape[2]
    width = col_embed.shape[2]
    row_index = lax.axis_index("row")
    col_index = lax.axis_index("col")
    half = row_index % 2
    home = row_index // 2

    mate_swap = [(i, i ^ 1) for i in range(8)]
    near_swap = [(i, i ^ 2) for i in range(8)]
    far_swap = [(i, i ^ 4) for i in range(8)]
    core_swap = [(i, i ^ 1) for i in range(4)]
    chip_swap = [(i, i ^ 2) for i in range(4)]

    def swap(name, value, axis, pairs):
        with jax.named_scope(name):
            return lax.ppermute(value, axis, pairs)

    chosen = block_cols[0, 0]
    mate_chosen = swap("mate_chosen", chosen, "row", mate_swap)
    seat = jnp.concatenate(
        [half[None], chosen, chosen ^ home, mate_chosen ^ home, col_index[None]]
    ).astype(jnp.int32)

    starts = [sum(CUTS[:part]) for part in range(len(CUTS))]

    def far_cols(part, own):
        far = swap(f"cols_far_{part}", own, "row", far_swap)
        return own, swap(f"cols_near_{part}", own, "row", near_swap), far

    def near_cols(part, own, near, far):
        return own, near, far, swap(f"cols_cross_{part}", far, "row", near_swap)

    cols = near_cols(0, *far_cols(0, col_embed[0, : CUTS[0] * LANES].astype(jnp.bfloat16)))
    row_half, done = halved(row_embed, 0, row_embed.shape[0], cols[:1])
    core_rows = swap("core_rows", row_half, "col", core_swap)
    chip_rows = swap("chip_rows", row_half, "col", chip_swap)
    both_rows = swap("both_rows", chip_rows, "col", core_swap)
    rows = (row_half, core_rows, chip_rows, both_rows)
    parts = len(CUTS)

    def own_cols(part, *tokens):
        if part >= parts:
            return None, tokens[0]
        return halved(col_embed, starts[part] * LANES, CUTS[part] * LANES, tokens)

    own_next, done = own_cols(1, done)
    coming = far_cols(1, *gated((own_next,), (*cols[1:3], done)))
    row_term = (jnp.log(row_freq.astype(jnp.float32)) - log_total)[:, None]

    def own(part, cols, done):
        *grads, col_grad, weight, target, done = own_grads(
            seat, row_term, col_freq, rows, cols, counts, starts[part], (done,)
        )
        return grads, col_grad, (weight, target), done

    def other(cols, terms, before, earlier, done):
        *grads, col_grad, done = other_grads(seat, rows, cols, *terms, before, earlier, (done,))
        return grads, col_grad, done

    row_grads, col_new, sent = [], (), None

    def pick_part(part, cols, coming, *tokens):
        if coming is not None:
            tokens += coming[2:]
        asked, kept, done = picked(seat, cols, slots, tokens)
        received = swap(f"cols_mate_{part}", asked, "row", mate_swap)
        after_next = None
        if coming is not None:
            cols = near_cols(part + 1, *coming[:2], *gated(coming[2:], (done,)))
            own_next, done = own_cols(part + 2, done)
            if own_next is not None:
                after_next = far_cols(part + 2, own_next)
        return kept, received, cols, after_next, done

    def sum_part(part, mine, from_mate, *tokens):
        split = part + 1 == parts
        home_sum, near, *rest, done = block_sums(seat, mine, from_mate, slots, split, tokens)
        count = len(rest) // 2
        cross = [
            swap(f"grads_cross_{part}_{i}", rest[count + i], "row", near_swap)
            for i in range(count)
        ]
        return (home_sum, near, rest[:count], cross), done

    def send_part(part, sums, *tokens):
        home_sum, near, (far,), (cross,) = sums
        far, done = relayed(far, cross, tokens)
        near = swap(f"grads_near_{part}", near, "row", near_swap)
        far = swap(f"grads_far_{part}", far, "row", far_swap)
        return (home_sum, near, far), done

    def update_part(start, sums, *tokens):
        *new, done = updated(col_embed, col_accum, start, sums, col_new, tokens)
        return new, done

    *_, cross = cols
    cols = (*cols[:3], *gated((cross,), (done,)))
    kept, received, cols, coming, done = pick_part(0, cols, coming, done, core_rows, chip_rows)
    for part in range(parts):
        own_rows, mine, terms, done = own(part, kept, done)
        if part + 1 < parts:
            kept, received_next, cols, coming, done = pick_part(
                part + 1, cols, coming, done
            )
        earlier = row_grads if part + 1 == parts else []
        other_rows, theirs, done = other(received, terms, own_rows, earlier, done)
        from_mate = swap(f"grads_mate_{part}", theirs, "row", mate_swap)
        if part:
            if sent:
                col_new, done = update_part(starts[part - 2], sent, done)
            sums, done = sum_part(part - 1, *waiting, done)
            if part + 1 == parts:
                home_grad, core_grad, chip_grad, both_grad = other_rows
                both_core = swap("row_grads_both", both_grad, "col", core_swap)
                from_core = swap("row_grads_core", core_grad, "col", core_swap)
            extra = (both_core,) if part + 1 == parts else ()
            sent, done = send_part(part - 1, sums, done, *extra)
        row_grads.append(other_rows)
        waiting = mine, from_mate
        received = received_next

    sums, done = sum_part(parts - 1, *waiting, done)
    chip_sum, row_done = added(chip_grad, both_core, (done,))
    from_chip = swap("row_grads_chip", chip_sum, "col", chip_swap)
    own_grad = home_grad + from_core + from_chip.astype(jnp.float32)
    row_new = row_updates(row_embed, row_accum, row_freq, excluded, block, own_grad)


    home_sum, near, fars, crosses = sums
    passed = gated(sent[:1], (*sent[1:], done)) if sent else ()
    far_sums = []
    for unit, (far, cross) in enumerate(zip(fars, crosses)):
        far, done = relayed(far, cross, (done, *passed))
        far_sums.append(swap(f"grads_far_{parts - 1}_{unit}", far, "row", far_swap))
    near = swap(f"grads_near_{parts - 1}", near, "row", near_swap)
    if sent:
        col_new, done = update_part(starts[parts - 2], (*passed, *sent[1:]), done)
    sums = home_sum, near, *far_sums
    col_new, done = update_part(starts[parts - 1], sums, done, row_new[1])
    return (*row_new, *col_new)


def row_updates(row_embed, row_accum, row_freq, excluded, block, own_grad):
    own_rows = row_embed.shape[0]
    col_index = lax.axis_index("col")
    row_index = lax.axis_index("row")
    own_freq = lax.dynamic_slice_in_dim(row_freq, col_index * own_rows, own_rows).astype(
        jnp.float32
    )
    row_ids = row_index * block + col_index * own_rows + jnp.arange(own_rows, dtype=jnp.int32)
    decayed = jnp.all(row_ids[:, None] != excluded[None, :], axis=1)
    freq_root = jnp.sqrt(own_freq)
    decay_coef = jnp.where(decayed, decay_rate * freq_root / (freq_root + 30.0), jnp.float32(0.0))
    full_grad = own_grad + decay_coef[:, None] * row_embed
    row_accum_new = row_accum + full_grad * full_grad
    row_embed_new = row_embed - learn_rate * full_grad / jnp.sqrt(row_accum_new)
    return row_embed_new, row_accum_new


def col_updates(col_embed, col_accum, col_grad):
    col_step = col_grad[None]
    col_accum_new = col_accum + col_step * col_step
    col_embed_new = col_embed - learn_rate * col_step / jnp.sqrt(col_accum_new)
    return col_embed_new, col_accum_new


def gathered_body(
    row_embed,
    row_accum,
    col_embed,
    col_accum,
    col_freq,
    row_freq,
    block_cols,
    counts,
    excluded,
    log_total,
):
    block = counts.shape[3]
    slots = counts.shape[2]
    width = row_embed.shape[1]
    chosen = block_cols[0, 0]
    block_rows = lax.all_gather(row_embed.astype(jnp.bfloat16), "col", axis=0, tiled=True)
    group = lax.all_gather(col_embed[0].astype(jnp.bfloat16), "row", axis=0, tiled=True)
    row_term = (jnp.log(row_freq.astype(jnp.float32)) - log_total)[:, None]
    col_logs = jnp.log(col_freq[0].astype(jnp.float32))
    row_grad = jnp.zeros((block, width), jnp.float32)
    summed = jnp.zeros(group.shape, jnp.float32)
    for slot in range(slots):
        start = chosen[slot] * block
        cols = lax.dynamic_slice_in_dim(group, start, block)
        predicted = lax.dot_general(
            block_rows, cols, (((1,), (1,)), ((), ())), preferred_element_type=jnp.float32
        )
        shifted = predicted + row_term + lax.dynamic_slice_in_dim(col_logs, start, block)[None]
        cell = cell_grads(counts[0, 0, slot], shifted, block)
        row_grad = row_grad + jnp.dot(cell, cols, preferred_element_type=jnp.float32)
        term = lax.dot_general(
            cell, block_rows, (((0,), (0,)), ((), ())), preferred_element_type=jnp.float32
        )
        summed = lax.dynamic_update_slice_in_dim(summed, term, start, 0)
    col_grad = lax.psum_scatter(summed, "row", scatter_dimension=0, tiled=True)
    own_grad = lax.psum_scatter(row_grad, "col", scatter_dimension=0, tiled=True)
    return (
        *row_updates(row_embed, row_accum, row_freq, excluded, block, own_grad),
        *col_updates(col_embed, col_accum, col_grad),
    )


def body(row_embed, row_accum, col_embed, col_accum, col_freq, row_freq, block_cols, counts, *rest):
    halves = lax.axis_size("row") == 8 and 2 * col_embed.shape[1] == counts.shape[3]
    pick = crossed_body if halves and lax.axis_size("col") == 4 else gathered_body
    return pick(
        row_embed, row_accum, col_embed, col_accum, col_freq, row_freq, block_cols, counts, *rest
    )


def solution(mesh):
    in_specs = (
        P(("row", "col"), None),
        P(("row", "col"), None),
        P("col", "row", None),
        P("col", "row", None),
        P("col", None),
        P("row"),
        P("row", "col", None),
        P("row", "col", None, None, None),
        P(),
        P(),
    )
    out_specs = (
        P(("row", "col"), None),
        P(("row", "col"), None),
        P("col", "row", None),
        P("col", "row", None),
    )
    return jax.shard_map(body, mesh=mesh, in_specs=in_specs, out_specs=out_specs, check_vma=False)
```
